256 devices in a mesh: dp: 32 (over z, y), mp: 8 (over x, core).
Axes of the slice: x: 4, y: 4, z: 8, core: 2. Of those that a mesh axis runs over, the one named last changes fastest.
Arguments:
- gradients: bfloat16 [32, 1536, 5120], P('dp', 'mp')
- errors: float32 [32, 1536, 5120], P('dp', 'mp'), may hold values from -3 to 3
- seed_table: int32 [5120, 32], replicated, may hold values from -1006 to 1006
Outputs:
- new_errors: float32 [32, 1536, 5120], P('dp', 'mp')
- update: bfloat16 [1536, 5120], P('mp')
- right_factor: float32 [5120, 32], replicated
- left_factor: float32 [1536, 32], P('mp')
The draws below stay inside these ranges and needn't reach their ends.
All inputs are finite; a program needn't handle non-finite values.
Results may differ from the reference program's by a relative error of at most 0.0015.
Values sent between devices are 32-bit elements; how exact they have to be, the bound alone decides.
A program may use at most 64 MiB of HBM per device.

```python
import math
import jax
import jax.numpy as jnp
from jax import lax

D = 5120
RANK = 32
FF = 1536
REPLICAS = 32


def draw_gradients(key, part):
    key = jax.random.fold_in(key, 11)
    key_col, key_shared, key_own = jax.random.split(key, 3)
    columns = jnp.exp(jax.random.uniform(key_col, (D,), jnp.float32, 0.0, math.log(10.0)))
    shared = jax.random.normal(key_shared, (FF, D), jnp.float32)
    own = jax.random.normal(key_own, (REPLICAS, FF, D), jnp.float32)
    result = 0.3 * (shared * columns[None, :])[None] + 0.5 * own
    return result.astype(jnp.bfloat16)


def draw_seed_table(key, part):
    key = jax.random.fold_in(key, 23)
    key_common, key_own, key_rows, key_cols = jax.random.split(key, 4)
    common = jax.random.randint(key_common, (D,), -1000, 1001, jnp.int32)
    own = jax.random.randint(key_own, (D, RANK), -6, 7, jnp.int32)
    chosen = jax.random.permutation(key_rows, D)[:2].astype(jnp.int32)
    picked = jax.random.randint(key_cols, (2,), 0, RANK, jnp.int32)
    common = common.at[chosen[0]].set(1000).at[chosen[1]].set(-1000)
    own = own.at[chosen[0], picked[0]].set(6).at[chosen[1], picked[1]].set(-6)
    return (common[:, None] + own).astype(jnp.int32)


def steps_of(stream_key, extent, pieces, least, largest):
    factor_of = 1.0
    for dim, blocks in pieces:
        heights = jax.random.uniform(jax.random.fold_in(jax.random.fold_in(stream_key, 6), dim), (blocks,), jnp.float32, least / len(pieces), largest / len(pieces))
        factor_of = factor_of * jnp.repeat(jnp.exp(heights), extent[dim] // blocks).reshape((-1,) + (1,) * (len(extent) - 1 - dim))
    return factor_of


def bell_draw(stream_key, extent, deviation, bound, pieces=(), kind=jnp.bfloat16):
    entries = deviation * jax.random.normal(stream_key, extent, jnp.float32)
    if pieces:
        entries = entries * steps_of(stream_key, extent, pieces, -0.22, 0.18)
    return jnp.clip(entries, -bound, bound).astype(kind)


def setup_inputs(seed: int = 0) -> dict:
    key_of = jax.random.split(jax.random.key(seed), 4)
    gradients = draw_gradients(jax.random.fold_in(key_of[3], 71), 0)
    errors = bell_draw(key_of[1], (REPLICAS, FF, D), 0.5, 3.0, ((0, 32), (1, 8)), jnp.float32)
    seed_table = draw_seed_table(jax.random.fold_in(key_of[3], 71), 0)
    return dict(gradients=gradients, errors=errors, seed_table=seed_table)


def orthonormal(left):
    gram_matrix = jnp.dot(left.T.astype(jnp.float32), left.astype(jnp.float32), precision=lax.Precision.HIGHEST, preferred_element_type=jnp.float32)
    lower = jnp.linalg.cholesky(gram_matrix)
    return jax.scipy.linalg.solve_triangular(lower, left.T, lower=True).T

def reference(gradients, errors, seed_table):
    start = seed_table.astype(jnp.float32) / 1000.0

    def left_step(total, pair):
        merged = pair[0].astype(jnp.float32) + pair[1]
        return (total + jnp.dot(merged.astype(jnp.float32), start.astype(jnp.float32), precision=lax.Precision.HIGHEST, preferred_element_type=jnp.float32), None)
    left0, _ = lax.scan(left_step, jnp.zeros((FF, RANK), jnp.float32), (gradients, errors))
    left_factor = orthonormal(orthonormal(left0))

    def right_step(total, pair):
        merged = pair[0].astype(jnp.float32) + pair[1]
        term = lax.dot_general(merged.astype(jnp.float32), left_factor.astype(jnp.float32), (((0,), (0,)), ((), ())), precision=lax.Precision.HIGHEST, preferred_element_type=jnp.float32)
        return (total + term, None)
    right_total, _ = lax.scan(right_step, jnp.zeros((D, RANK), jnp.float32), (gradients, errors))
    right_factor = right_total / REPLICAS
    approx = jnp.dot(left_factor.astype(jnp.float32), right_factor.T.astype(jnp.float32), precision=lax.Precision.HIGHEST, preferred_element_type=jnp.float32)

    def error_step(pair):
        return pair[0].astype(jnp.float32) + pair[1] - approx
    new_errors = lax.map(error_step, (gradients, errors))
    return (new_errors, approx.astype(jnp.bfloat16), right_factor, left_factor)
```

```python
import functools

import jax
import jax.numpy as jnp
from jax import lax
from jax.experimental import pallas as pl
from jax.experimental.pallas import tpu as pltpu
from jax.sharding import PartitionSpec as P

MESH = pl.DeviceIdType.MESH
F32, BF16 = jnp.float32, jnp.bfloat16
HIGHEST = lax.Precision.HIGHEST

ROWS, COLS, RANK = 192, 5120, 32
DP, MP, XS, YS = 32, 8, 4, 4
PARTS = 8
WIDE = COLS // PARTS
TILES = (RANK // 8) * (WIDE // 128)
ROW_TILES = 8


def split(value, parts):
    out = []
    for _ in range(parts):
        piece = value.astype(BF16)
        out.append(piece)
        value = value - piece.astype(F32)
    return out


def dot(a, b):
    return jnp.dot(a, b, preferred_element_type=F32)


def full_dot(a, b, dims=((1,), (0,))):
    return lax.dot_general(a, b, (dims, ((), ())), precision=HIGHEST, preferred_element_type=F32)


def inverse_cholesky(gram):
    row_id = lax.broadcasted_iota(jnp.int32, (RANK, 128), 0)
    lane_id = lax.broadcasted_iota(jnp.int32, (RANK, 128), 1)
    table = jnp.concatenate([gram, jnp.zeros((RANK, 128 - RANK), F32)], axis=1)
    table = table + jnp.where(lane_id == row_id + RANK, 1.0, 0.0)
    for j in range(RANK - 1):
        row = table[j : j + 1, :] / table[j : j + 1, j : j + 1]
        column = jnp.where(row_id > j, table[:, j : j + 1], 0.0)
        table = table - column * row
    pivots = jnp.sum(jnp.where(lane_id == row_id, table, 0.0), axis=1, keepdims=True)
    return table[:, RANK : 2 * RANK] / jnp.sqrt(pivots)


def pack(gram):
    return jnp.concatenate([gram[8 * s : 8 * s + 8, :] for s in range(4)], axis=1)


def unpack(tile):
    return jnp.concatenate([tile[:, 32 * s : 32 * s + 32] for s in range(4)], axis=0)


def exchange(
    g_hbm, e_hbm, seed_hbm, right_ref, mix_ref, left_ref,
    g_buf, e_buf, seed_buf, start, merged,
    left_tiles, left_in, left_all,
    gram_in, gram_in2,
    core_out, core_in, own, x_in, sum_tiles, dp_in, full,
    load_sem, seed_sem,
    lt_send, lt_recv, la_send, la_recv, gr_send, gr_recv,
    core_send, core_recv, x_send, x_recv, dp_send, dp_recv, dg_send, dg_recv,
    ax_send, ax_recv, ac_send, ac_recv,
):
    me = lax.axis_index("dp")
    mp = lax.axis_index("mp")
    z, y = me // YS, me % YS
    x, core = mp // 2, mp % 2
    sibling = (me, x * 2 + 1 - core)

    seed_copy = pltpu.make_async_copy(seed_hbm, seed_buf, seed_sem)
    seed_copy.start()
    loads = []
    for i in range(PARTS):
        columns = pl.ds(i * WIDE, WIDE)
        pair = (
            pltpu.make_async_copy(g_hbm.at[:, columns], g_buf.at[i], load_sem.at[0, i]),
            pltpu.make_async_copy(e_hbm.at[:, columns], e_buf.at[i], load_sem.at[1, i]),
        )
        for copy in pair:
            copy.start()
        loads.append(pair)

    barrier = pltpu.get_barrier_semaphore()

    @pl.loop(1, DP)
    def _(k):
        pl.semaphore_signal(barrier, inc=1, device_id=(lax.rem(me + k, DP), mp), device_id_type=MESH)

    @pl.loop(1, MP)
    def _(k):
        pl.semaphore_signal(barrier, inc=1, device_id=(me, lax.rem(mp + k, MP)), device_id_type=MESH)

    seed_copy.wait()
    seeds = seed_buf[...].astype(F32) * (1.0 / 1024.0)
    less = seeds - seeds[0:1, :]
    shorter = jnp.sum(less * less, axis=1, keepdims=True) < jnp.sum(seeds * seeds, axis=1, keepdims=True)
    first = lax.broadcasted_iota(jnp.int32, (RANK, 1), 0) == 0
    take = jnp.where(jnp.logical_and(shorter, jnp.logical_not(first)), 1.0, 0.0)
    seeds = seeds - take * seeds[0:1, :]
    high, low = split(seeds, 2)
    blank = jnp.zeros((64, WIDE), BF16)
    for i in range(PARTS):
        columns = slice(i * WIDE, (i + 1) * WIDE)
        start[i] = jnp.concatenate([high[:, columns], low[:, columns], blank], axis=0)

    total = jnp.zeros((2 * ROWS, 128), F32)
    for i in range(PARTS):
        for copy in loads[i]:
            copy.wait()
        both = g_buf[i].astype(F32) + e_buf[i]
        upper, lower = split(both, 2)
        merged[i, 0:ROWS, :] = upper
        merged[i, ROWS : 2 * ROWS, :] = lower
        total = total + lax.dot_general(
            merged[i], start[i], (((1,), (1,)), ((), ())), preferred_element_type=F32
        )
    left = total[0:ROWS] + total[ROWS : 2 * ROWS]
    turned = jnp.transpose(jnp.concatenate([left, jnp.zeros((64, 128), F32)], axis=0))
    left = (turned[0:RANK] + turned[RANK : 2 * RANK]) * 1.024
    for t in range(2):
        for s in range(4):
            left_tiles[4 * t + s] = left[8 * s : 8 * s + 8, 128 * t : 128 * t + 128]

    pl.semaphore_wait(barrier, DP + MP - 2)

    def remote(src, dst, send, recv, device):
        return pltpu.make_async_remote_copy(
            src_ref=src, dst_ref=dst, send_sem=send, recv_sem=recv, device_id=device, device_id_type=MESH
        )

    def wait_bytes(ref, sem):
        pltpu.make_async_copy(ref, ref, sem).wait()

    left_owner = y == lax.rem(z, YS)

    @pl.loop(0, ROW_TILES)
    def _(k):
        tile = lax.rem(z + k, ROW_TILES)
        owner = tile * YS + lax.rem(tile, YS)

        @pl.when(owner != me)
        def _():
            remote(left_tiles.at[tile], left_in.at[me], lt_send, lt_recv, (owner, mp)).start()

    @pl.when(left_owner)
    def _():
        left_in[me] = left_tiles[z]
        wait_bytes(left_in.at[pl.ds(0, DP - 1)], lt_recv)
        left_all[z] = jnp.sum(left_in[...], axis=0)

        @pl.loop(1, DP)
        def _(k):
            remote(left_all.at[z], left_all.at[z], la_send, la_recv, (lax.rem(me + k, DP), mp)).start()

        wait_bytes(left_all.at[pl.ds(0, ROW_TILES - 1)], la_recv)

    @pl.when(jnp.logical_not(left_owner))
    def _():
        wait_bytes(left_all.at[pl.ds(0, ROW_TILES)], la_recv)

    left0 = jnp.concatenate(
        [jnp.concatenate([left_all[4 * t + s] for s in range(4)], axis=0) for t in range(2)], axis=1
    )

    def send_gram(slots, which, value):
        slots[mp] = pack(full_dot(value, value, ((1,), (1,))))

        @pl.loop(1, MP)
        def _(k):
            remote(
                slots.at[mp], slots.at[mp], gr_send.at[which], gr_recv.at[which], (me, lax.rem(mp + k, MP))
            ).start()

    def take_gram(slots, which):
        wait_bytes(slots.at[pl.ds(0, MP - 1)], gr_recv.at[which])
        return unpack(jnp.sum(slots[...], axis=0))

    send_gram(gram_in, 0, left0)

    pieces = jnp.concatenate(split(left0[:, 0:ROWS], 3), axis=0)

    def right_part(part):
        one = dot(pieces, merged[part, 0:ROWS, :])
        two = dot(pieces[0 : 2 * RANK], merged[part, ROWS : 2 * ROWS, :])
        return (one[0:32] + (one[32:64] + two[0:32])) + (one[64:96] + two[32:64])

    order = (2, 1, 3, 0)
    for k in order:
        core_out[k] = right_part((1 - core) * XS + lax.rem(x + k, XS))
        remote(core_out.at[k], core_in.at[k], core_send, core_recv.at[k], sibling).start()
    for k in order:
        own[k] = right_part(core * XS + lax.rem(x + k, XS))
    for k in order:
        wait_bytes(core_in.at[k], core_recv.at[k])
        own[k] = own[k] + core_in[k]
        if k:
            target = (me, lax.rem(x + k, XS) * 2 + core)
            remote(own.at[k], x_in.at[k - 1], x_send, x_recv.at[k - 1], target).start()

    inverse1 = inverse_cholesky(take_gram(gram_in, 0))
    left1 = full_dot(inverse1, left0)
    send_gram(gram_in2, 1, left1)

    for k in range(1, XS):
        wait_bytes(x_in.at[k - 1], x_recv.at[k - 1])
    sums = (own[0] + x_in[0]) + (x_in[1] + x_in[2])
    for t in range(WIDE // 128):
        for s in range(4):
            sum_tiles[4 * t + s] = sums[8 * s : 8 * s + 8, 128 * t : 128 * t + 128]

    mine = core * XS + x
    owns = me < TILES

    @pl.loop(1, DP)
    def _(k):
        owner = lax.rem(me + k, DP)

        @pl.when(owner < TILES)
        def _():
            remote(sum_tiles.at[owner], dp_in.at[me], dp_send, dp_recv, (owner, mp)).start()

    @pl.when(owns)
    def _():
        dp_in[me] = sum_tiles[me]
        wait_bytes(dp_in.at[pl.ds(0, DP - 1)], dp_recv)
        full[mine, me] = jnp.sum(dp_in[...], axis=0)

        @pl.loop(1, DP)
        def _(k):
            remote(
                full.at[mine, me], full.at[mine, me], dg_send, dg_recv, (lax.rem(me + k, DP), mp)
            ).start()

        wait_bytes(full.at[0, pl.ds(0, TILES - 1)], dg_recv)

    @pl.when(jnp.logical_not(owns))
    def _():
        wait_bytes(full.at[0], dg_recv)

    for k in range(1, XS):
        target = (me, lax.rem(x + k, XS) * 2 + core)
        remote(full.at[mine], full.at[mine], ax_send, ax_recv.at[k - 1], target).start()
    remote(full.at[mine], full.at[mine], ac_send, ac_recv.at[0], sibling).start()

    inverse2 = inverse_cholesky(take_gram(gram_in2, 1))
    left_ref[...] = full_dot(inverse2, left1)[:, 0:ROWS]
    mix_ref[...] = full_dot(inverse2, inverse1)

    for k in (1, 3, 2):
        got = core * XS + lax.rem(x + XS - k, XS)
        wait_bytes(full.at[0], ax_recv.at[k - 1])
        remote(full.at[got], full.at[got], ac_send, ac_recv.at[k], sibling).start()
    for k in range(XS):
        wait_bytes(full.at[0], ac_recv.at[k])
    right_ref[...] = full[...]

    @pl.when(left_owner)
    def _():
        wait_bytes(left_in.at[pl.ds(0, ROW_TILES - 1)], lt_send)
        wait_bytes(left_in.at[pl.ds(0, DP - 1)], la_send)

    @pl.when(jnp.logical_not(left_owner))
    def _():
        wait_bytes(left_in.at[pl.ds(0, ROW_TILES)], lt_send)

    for which in range(2):
        wait_bytes(left_in.at[pl.ds(0, MP - 1)], gr_send.at[which])

    @pl.when(owns)
    def _():
        wait_bytes(dp_in.at[pl.ds(0, TILES - 1)], dp_send)
        wait_bytes(dp_in.at[pl.ds(0, DP - 1)], dg_send)

    @pl.when(jnp.logical_not(owns))
    def _():
        wait_bytes(dp_in.at[pl.ds(0, TILES)], dp_send)

    wait_bytes(core_out, core_send)
    wait_bytes(x_in, x_send)
    wait_bytes(x_in, ax_send)
    wait_bytes(core_out, ac_send)


def run_exchange(gradients, errors, seeds):
    hbm = pl.BlockSpec(memory_space=pl.ANY)
    vmem = pl.BlockSpec(memory_space=pltpu.VMEM)
    dma = pltpu.SemaphoreType.DMA
    return pl.pallas_call(
        exchange,
        out_shape=(
            jax.ShapeDtypeStruct((PARTS, TILES, 8, 128), F32),
            jax.ShapeDtypeStruct((RANK, RANK), F32),
            jax.ShapeDtypeStruct((RANK, ROWS), F32),
        ),
        in_specs=[hbm, hbm, hbm],
        out_specs=(vmem, vmem, vmem),
        scratch_shapes=[
            pltpu.VMEM((PARTS, ROWS, WIDE), BF16),
            pltpu.VMEM((PARTS, ROWS, WIDE), F32),
            pltpu.VMEM((RANK, COLS), jnp.int32),
            pltpu.VMEM((PARTS, 128, WIDE), BF16),
            pltpu.VMEM((PARTS, 2 * ROWS, WIDE), BF16),
            pltpu.VMEM((ROW_TILES, 8, 128), F32),
            pltpu.VMEM((DP, 8, 128), F32),
            pltpu.VMEM((ROW_TILES, 8, 128), F32),
            pltpu.VMEM((MP, 8, 128), F32),
            pltpu.VMEM((MP, 8, 128), F32),
            pltpu.VMEM((XS, RANK, WIDE), F32),
            pltpu.VMEM((XS, RANK, WIDE), F32),
            pltpu.VMEM((XS, RANK, WIDE), F32),
            pltpu.VMEM((XS - 1, RANK, WIDE), F32),
            pltpu.VMEM((TILES, 8, 128), F32),
            pltpu.VMEM((DP, 8, 128), F32),
            pltpu.VMEM((PARTS, TILES, 8, 128), F32),
            dma((2, PARTS)),
            dma,
            dma, dma, dma, dma, dma((2,)), dma((2,)),
            dma, dma((XS,)), dma, dma((XS - 1,)), dma, dma, dma, dma,
            dma, dma((XS - 1,)), dma, dma((XS,)),
        ],
        compiler_params=pltpu.CompilerParams(
            collective_id=0, has_side_effects=True, vmem_limit_bytes=40 * 1024 * 1024
        ),
        cost_estimate=pl.CostEstimate(flops=10**9, bytes_accessed=8 * 10**6, transcendentals=0),
        name="exchange",
    )(gradients, errors, seeds)


def finish(g_ref, e_ref, sums_ref, mix_ref, left_ref, new_ref, update_ref, right_ref, left_out):
    def stack_left(value):
        h, m, l = [p.astype(F32) for p in split(value, 3)]
        return jnp.concatenate([h, h, m, m, h, l], axis=0)

    def stack_right(value):
        h, m, l = split(value, 3)
        return jnp.concatenate([h, m, h, m, l, h], axis=0)

    mix = mix_ref[...]
    mix_t = jnp.concatenate([jnp.transpose(jnp.pad(mix, ((0, 96), (0, 96))))[0:32]], axis=0)
    mix_wide = jnp.transpose(stack_left(mix_t)).astype(BF16)
    left = left_ref[...]
    left_wide = jnp.transpose(stack_left(left)).astype(BF16)
    for part in range(sums_ref.shape[0]):
        columns = slice(part * WIDE, (part + 1) * WIDE)
        sums = jnp.concatenate(
            [
                jnp.concatenate([sums_ref[part, 4 * t + s] for s in range(4)], axis=0)
                for t in range(WIDE // 128)
            ],
            axis=1,
        )
        right = dot(mix_wide, stack_right(sums))[0:RANK] * (1.0 / DP)
        right_ref[:, columns] = right
        approx = dot(left_wide, stack_right(right))
        update_ref[:, columns] = approx.astype(BF16)
        new_ref[:, columns] = (g_ref[:, columns].astype(F32) + e_ref[:, columns]) - approx
    left_out[...] = left


def run_finish(gradients, errors, sums, mix, left):
    parts = 2
    wide = parts * WIDE
    columns = lambda rows: pl.BlockSpec((rows, wide), lambda i: (0, i))
    whole = lambda *shape: pl.BlockSpec(shape, lambda i: (0,) * len(shape))
    return pl.pallas_call(
        finish,
        grid=(PARTS // parts,),
        out_shape=(
            jax.ShapeDtypeStruct((ROWS, COLS), F32),
            jax.ShapeDtypeStruct((ROWS, COLS), BF16),
            jax.ShapeDtypeStruct((RANK, COLS), F32),
            jax.ShapeDtypeStruct((RANK, ROWS), F32),
        ),
        in_specs=[
            columns(ROWS),
            columns(ROWS),
            pl.BlockSpec((parts, TILES, 8, 128), lambda i: (i, 0, 0, 0)),
            whole(RANK, RANK),
            whole(RANK, ROWS),
        ],
        out_specs=(columns(ROWS), columns(ROWS), columns(RANK), whole(RANK, ROWS)),
        compiler_params=pltpu.CompilerParams(vmem_limit_bytes=40 * 1024 * 1024),
        cost_estimate=pl.CostEstimate(flops=10**9, bytes_accessed=14 * 10**6, transcendentals=0),
        name="finish",
    )(gradients, errors, sums, mix, left)


def local(gradients, errors, seed_table):
    sums, mix, left = run_exchange(gradients[0], errors[0], seed_table.T)
    new_errors, update, right, left = run_finish(gradients[0], errors[0], sums, mix, left)
    return (new_errors[None], update, right.T, left.T)


def solution(mesh):
    in_specs = (P("dp", "mp", None), P("dp", "mp", None), P())
    out_specs = (P("dp", "mp", None), P("mp", None), P(), P("mp", None))
    return jax.shard_map(local, mesh=mesh, in_specs=in_specs, out_specs=out_specs, check_vma=False)
```

```python
import jax
import jax.numpy as jnp
from jax import lax
from jax.experimental import pallas as pl
from jax.experimental.pallas import tpu as pltpu
from jax.sharding import PartitionSpec as P

MESH = pl.DeviceIdType.MESH
F32, BF16 = jnp.float32, jnp.bfloat16
HIGHEST = lax.Precision.HIGHEST

ROWS, COLS, RANK = 192, 5120, 32
DP, MP, XS, YS = 32, 8, 4, 4
PARTS = 8
WIDE = COLS // PARTS
ROW_TILES = 8


def split(value, parts):
    out = []
    for _ in range(parts):
        piece = value.astype(BF16)
        out.append(piece)
        value = value - piece.astype(F32)
    return out


def dot(a, b):
    return jnp.dot(a, b, preferred_element_type=F32)


def full_dot(a, b, dims=((1,), (0,))):
    return lax.dot_general(a, b, (dims, ((), ())), precision=HIGHEST, preferred_element_type=F32)


def inverse_cholesky(gram):
    row_id = lax.broadcasted_iota(jnp.int32, (RANK, 128), 0)
    lane_id = lax.broadcasted_iota(jnp.int32, (RANK, 128), 1)
    table = jnp.concatenate([gram, jnp.zeros((RANK, 128 - RANK), F32)], axis=1)
    table = table + jnp.where(lane_id == row_id + RANK, 1.0, 0.0)
    for j in range(RANK - 1):
        row = table[j : j + 1, :] / table[j : j + 1, j : j + 1]
        column = jnp.where(row_id > j, table[:, j : j + 1], 0.0)
        table = table - column * row
    pivots = jnp.sum(jnp.where(lane_id == row_id, table, 0.0), axis=1, keepdims=True)
    return table[:, RANK : 2 * RANK] / jnp.sqrt(pivots)


def pack(gram):
    return jnp.concatenate([gram[8 * s : 8 * s + 8, :] for s in range(4)], axis=1)


def unpack(tile):
    return jnp.concatenate([tile[:, 32 * s : 32 * s + 32] for s in range(4)], axis=0)


def stack_left(value):
    h, m, l = [p.astype(F32) for p in split(value, 3)]
    return jnp.concatenate([h, h, m, m, h, l], axis=0)


def stack_right(value):
    h, m, l = split(value, 3)
    return jnp.concatenate([h, m, h, m, l, h], axis=0)


def exchange(
    g_hbm, e_hbm, seed_hbm, both_ref, right_ref, wide_ref, left_ref,
    g_buf, e_buf, seed_buf, start, merged,
    left_tiles, left_in, left_all,
    gram_in, gram_in2,
    core_out, core_in, own, xy_in, z_in, full,
    load_sem, seed_sem,
    lt_send, lt_recv, la_send, la_recv, gr_send, gr_recv,
    core_send, core_recv, xy_send, xy_recv, z_send, z_recv,
    ag_send, ag_recv, ac_send, ac_recv,
):
    me = lax.axis_index("dp")
    mp = lax.axis_index("mp")
    z, y = me // YS, me % YS
    x, core = mp // 2, mp % 2
    sibling = (me, x * 2 + 1 - core)

    def plane(kx, ky):
        return (z * YS + lax.rem(y + ky, YS), lax.rem(x + kx, XS) * 2 + core)

    seed_copy = pltpu.make_async_copy(seed_hbm, seed_buf, seed_sem)
    seed_copy.start()
    loads = []
    for i in range(PARTS):
        columns = pl.ds(i * WIDE, WIDE)
        pair = (
            pltpu.make_async_copy(g_hbm.at[:, columns], g_buf.at[i], load_sem.at[0, i]),
            pltpu.make_async_copy(e_hbm.at[:, columns], e_buf.at[i], load_sem.at[1, i]),
        )
        for copy in pair:
            copy.start()
        loads.append(pair)

    barrier = pltpu.get_barrier_semaphore()

    @pl.loop(1, DP)
    def _(k):
        pl.semaphore_signal(barrier, inc=1, device_id=(lax.rem(me + k, DP), mp), device_id_type=MESH)

    @pl.loop(1, MP)
    def _(k):
        pl.semaphore_signal(barrier, inc=1, device_id=(me, lax.rem(mp + k, MP)), device_id_type=MESH)

    for kx in range(1, XS):
        for ky in range(1, YS):
            pl.semaphore_signal(barrier, inc=1, device_id=plane(kx, ky), device_id_type=MESH)

    seed_copy.wait()
    seeds = seed_buf[...].astype(F32) * (1.0 / 1024.0)
    less = seeds - seeds[0:1, :]
    shorter = jnp.sum(less * less, axis=1, keepdims=True) < jnp.sum(seeds * seeds, axis=1, keepdims=True)
    first = lax.broadcasted_iota(jnp.int32, (RANK, 1), 0) == 0
    take = jnp.where(jnp.logical_and(shorter, jnp.logical_not(first)), 1.0, 0.0)
    seeds = seeds - take * seeds[0:1, :]
    high, low = split(seeds, 2)
    blank = jnp.zeros((64, WIDE), BF16)
    for i in range(PARTS):
        columns = slice(i * WIDE, (i + 1) * WIDE)
        start[i] = jnp.concatenate([high[:, columns], low[:, columns], blank], axis=0)

    total = jnp.zeros((2 * ROWS, 128), F32)
    for i in range(PARTS):
        for copy in loads[i]:
            copy.wait()
        both = g_buf[i].astype(F32) + e_buf[i]
        both_ref[i] = both
        upper, lower = split(both, 2)
        merged[i, 0:ROWS, :] = upper
        merged[i, ROWS : 2 * ROWS, :] = lower
        total = total + lax.dot_general(
            merged[i], start[i], (((1,), (1,)), ((), ())), preferred_element_type=F32
        )
    left = total[0:ROWS] + total[ROWS : 2 * ROWS]
    turned = jnp.transpose(jnp.concatenate([left, jnp.zeros((64, 128), F32)], axis=0))
    left = (turned[0:RANK] + turned[RANK : 2 * RANK]) * 1.024
    for t in range(2):
        for s in range(4):
            left_tiles[4 * t + s] = left[8 * s : 8 * s + 8, 128 * t : 128 * t + 128]

    pl.semaphore_wait(barrier, DP + MP - 2 + (XS - 1) * (YS - 1))

    def remote(src, dst, send, recv, device):
        return pltpu.make_async_remote_copy(
            src_ref=src, dst_ref=dst, send_sem=send, recv_sem=recv, device_id=device, device_id_type=MESH
        )

    def wait_bytes(ref, sem):
        pltpu.make_async_copy(ref, ref, sem).wait()

    left_owner = y == lax.rem(z, YS)

    @pl.loop(0, ROW_TILES)
    def _(k):
        tile = lax.rem(z + k, ROW_TILES)
        owner = tile * YS + lax.rem(tile, YS)

        @pl.when(owner != me)
        def _():
            remote(left_tiles.at[tile], left_in.at[me], lt_send, lt_recv, (owner, mp)).start()

    @pl.when(left_owner)
    def _():
        left_in[me] = left_tiles[z]
        wait_bytes(left_in.at[pl.ds(0, DP - 1)], lt_recv)
        left_all[z] = jnp.sum(left_in[...], axis=0)

        @pl.loop(1, DP)
        def _(k):
            remote(left_all.at[z], left_all.at[z], la_send, la_recv, (lax.rem(me + k, DP), mp)).start()

        wait_bytes(left_all.at[pl.ds(0, ROW_TILES - 1)], la_recv)

    @pl.when(jnp.logical_not(left_owner))
    def _():
        wait_bytes(left_all.at[pl.ds(0, ROW_TILES)], la_recv)

    left0 = jnp.concatenate(
        [jnp.concatenate([left_all[4 * t + s] for s in range(4)], axis=0) for t in range(2)], axis=1
    )

    def send_gram(slots, which, value):
        slots[mp] = pack(full_dot(value, value, ((1,), (1,))))

        @pl.loop(1, MP)
        def _(k):
            remote(
                slots.at[mp], slots.at[mp], gr_send.at[which], gr_recv.at[which], (me, lax.rem(mp + k, MP))
            ).start()

    def take_gram(slots, which):
        wait_bytes(slots.at[pl.ds(0, MP - 1)], gr_recv.at[which])
        return unpack(jnp.sum(slots[...], axis=0))

    send_gram(gram_in, 0, left0)

    pieces = jnp.concatenate(split(left0[:, 0:ROWS], 3), axis=0)

    def right_part(into, part):
        one = dot(pieces, merged[part, 0:ROWS, :])
        two = dot(pieces[0 : 2 * RANK], merged[part, ROWS : 2 * ROWS, :])
        value = (one[0:32] + (one[32:64] + two[0:32])) + (one[64:96] + two[32:64])
        for s in range(YS):
            into[s] = value[8 * s : 8 * s + 8]

    order = (2, 1, 3, 0)
    for k in order:
        right_part(core_out.at[k], (1 - core) * XS + lax.rem(x + k, XS))
        remote(core_out.at[k], core_in.at[k], core_send, core_recv.at[k], sibling).start()
    for k in order:
        right_part(own.at[k], core * XS + lax.rem(x + k, XS))

    for kx in order:
        wait_bytes(core_in.at[kx], core_recv.at[kx])
        own[kx] = own[kx] + core_in[kx]
        for ky in (2, 1, 3, 0):
            if kx or ky:
                slot = kx * YS + ky - 1
                remote(
                    own.at[kx, lax.rem(y + ky, YS)], xy_in.at[slot], xy_send, xy_recv, plane(kx, ky)
                ).start()

    inverse1 = inverse_cholesky(take_gram(gram_in, 0))
    left1 = full_dot(inverse1, left0)
    send_gram(gram_in2, 1, left1)

    wait_bytes(xy_in, xy_recv)
    z_in[z] = own[0, y] + jnp.sum(xy_in[...], axis=0)

    @pl.loop(1, ROW_TILES)
    def _(k):
        remote(z_in.at[z], z_in.at[z], z_send, z_recv, (lax.rem(z + k, 8) * YS + y, mp)).start()

    inverse2 = inverse_cholesky(take_gram(gram_in2, 1))
    left2 = full_dot(inverse2, left1)[:, 0:ROWS]
    left_ref[...] = left2
    wide_ref[...] = jnp.transpose(stack_left(left2)).astype(BF16)
    mix = full_dot(inverse2, inverse1)
    mix = jnp.transpose(jnp.pad(mix, ((0, 96), (0, 96))))[0:RANK]
    mix = jnp.transpose(stack_left(mix)).astype(BF16)[0:RANK]

    mine = core * XS + x
    wait_bytes(z_in.at[pl.ds(0, 7)], z_recv)
    full[mine, y] = jnp.sum(z_in[...], axis=0)
    for kx in order:
        for ky in (2, 1, 3, 0):
            if kx or ky:
                remote(full.at[mine, y], full.at[mine, y], ag_send, ag_recv.at[kx], plane(kx, ky)).start()

    def right_of(part):
        sums = jnp.concatenate([full[part, s] for s in range(4)], axis=0)
        right_ref[part] = dot(mix, stack_right(sums)) * (1.0 / DP)

    for kx in (0, 1, 3, 2):
        got = core * XS + lax.rem(x + XS - kx, XS)
        wait_bytes(full.at[0, pl.ds(0, YS if kx else YS - 1)], ag_recv.at[kx])
        remote(full.at[got], full.at[got], ac_send, ac_recv.at[kx], sibling).start()
        right_of(got)
    for kx in (0, 1, 3, 2):
        wait_bytes(full.at[0], ac_recv.at[kx])
        right_of((1 - core) * XS + lax.rem(x + XS - kx, XS))

    @pl.when(left_owner)
    def _():
        wait_bytes(left_in.at[pl.ds(0, ROW_TILES - 1)], lt_send)
        wait_bytes(left_in.at[pl.ds(0, DP - 1)], la_send)

    @pl.when(jnp.logical_not(left_owner))
    def _():
        wait_bytes(left_in.at[pl.ds(0, ROW_TILES)], lt_send)

    for which in range(2):
        wait_bytes(left_in.at[pl.ds(0, MP - 1)], gr_send.at[which])
    wait_bytes(core_out, core_send)
    wait_bytes(xy_in, xy_send)
    wait_bytes(z_in.at[pl.ds(0, 7)], z_send)
    wait_bytes(xy_in, ag_send)
    wait_bytes(core_out, ac_send)


def run_exchange(gradients, errors, seeds):
    hbm = pl.BlockSpec(memory_space=pltpu.HBM)
    vmem = pl.BlockSpec(memory_space=pltpu.VMEM)
    dma = pltpu.SemaphoreType.DMA
    return pl.pallas_call(
        exchange,
        out_shape=(
            jax.ShapeDtypeStruct((PARTS, ROWS, WIDE), F32),
            jax.ShapeDtypeStruct((PARTS, RANK, WIDE), F32),
            jax.ShapeDtypeStruct((ROWS, 6 * RANK), BF16),
            jax.ShapeDtypeStruct((RANK, ROWS), F32),
        ),
        in_specs=[hbm, hbm, hbm],
        out_specs=(vmem,) * 4,
        scratch_shapes=[
            pltpu.VMEM((PARTS, ROWS, WIDE), BF16),
            pltpu.VMEM((PARTS, ROWS, WIDE), F32),
            pltpu.VMEM((RANK, COLS), jnp.int32),
            pltpu.VMEM((PARTS, 128, WIDE), BF16),
            pltpu.VMEM((PARTS, 2 * ROWS, WIDE), BF16),
            pltpu.VMEM((ROW_TILES, 8, 128), F32),
            pltpu.VMEM((DP, 8, 128), F32),
            pltpu.VMEM((ROW_TILES, 8, 128), F32),
            pltpu.VMEM((MP, 8, 128), F32),
            pltpu.VMEM((MP, 8, 128), F32),
            pltpu.VMEM((XS, YS, 8, WIDE), F32),
            pltpu.VMEM((XS, YS, 8, WIDE), F32),
            pltpu.VMEM((XS, YS, 8, WIDE), F32),
            pltpu.VMEM((XS * YS - 1, 8, WIDE), F32),
            pltpu.VMEM((DP // YS, 8, WIDE), F32),
            pltpu.VMEM((PARTS, YS, 8, WIDE), F32),
            dma((2, PARTS)),
            dma,
            dma, dma, dma, dma, dma((2,)), dma((2,)),
            dma, dma((XS,)), dma, dma, dma, dma,
            dma, dma((XS,)), dma, dma((XS,)),
        ],
        compiler_params=pltpu.CompilerParams(
            collective_id=0, has_side_effects=True, vmem_limit_bytes=40 * 1024 * 1024
        ),
        cost_estimate=pl.CostEstimate(flops=10**9, bytes_accessed=8 * 10**6, transcendentals=0),
        name="exchange",
    )(*(pltpu.with_memory_space_constraint(v, pltpu.HBM) for v in (gradients, errors, seeds)))


def finish(
    both_ref, right_ref, wide_ref, left_ref, new_hbm, update_hbm, right_hbm, left_hbm,
    new_buf, update_buf, new_sem, update_sem, right_sem, left_sem,
):
    copies = [pltpu.make_async_copy(left_ref, left_hbm, left_sem)]
    copies[0].start()
    for part in range(PARTS):
        columns = pl.ds(part * WIDE, WIDE)
        approx = dot(wide_ref[...], stack_right(right_ref[part]))
        new_buf[part] = both_ref[part] - approx
        update_buf[part] = approx.astype(BF16)
        for copy in (
            pltpu.make_async_copy(new_buf.at[part], new_hbm.at[:, columns], new_sem.at[part]),
            pltpu.make_async_copy(update_buf.at[part], update_hbm.at[:, columns], update_sem.at[part]),
            pltpu.make_async_copy(right_ref.at[part], right_hbm.at[:, columns], right_sem.at[part]),
        ):
            copy.start()
            copies.append(copy)
    for copy in copies:
        copy.wait()


def run_finish(*operands):
    hbm = pl.BlockSpec(memory_space=pltpu.HBM)
    vmem = pl.BlockSpec(memory_space=pltpu.VMEM)
    dma = pltpu.SemaphoreType.DMA
    return pl.pallas_call(
        finish,
        out_shape=(
            jax.ShapeDtypeStruct((ROWS, COLS), F32),
            jax.ShapeDtypeStruct((ROWS, COLS), BF16),
            jax.ShapeDtypeStruct((RANK, COLS), F32),
            jax.ShapeDtypeStruct((RANK, ROWS), F32),
        ),
        in_specs=[vmem] * 4,
        out_specs=(hbm,) * 4,
        scratch_shapes=[
            pltpu.VMEM((PARTS, ROWS, WIDE), F32),
            pltpu.VMEM((PARTS, ROWS, WIDE), BF16),
            dma((PARTS,)), dma((PARTS,)), dma((PARTS,)), dma,
        ],
        compiler_params=pltpu.CompilerParams(vmem_limit_bytes=40 * 1024 * 1024),
        cost_estimate=pl.CostEstimate(flops=10**9, bytes_accessed=10**7, transcendentals=0),
        name="finish",
    )(*operands)


def local(gradients, errors, seed_table):
    new_errors, update, right, left = run_finish(*run_exchange(gradients[0], errors[0], seed_table.T))
    return (new_errors[None], update, right.T, left.T)


def solution(mesh):
    in_specs = (P("dp", "mp", None), P("dp", "mp", None), P())
    out_specs = (P("dp", "mp", None), P("mp", None), P(), P("mp", None))
    return jax.shard_map(local, mesh=mesh, in_specs=in_specs, out_specs=out_specs, check_vma=False)
```

```python
import jax
import jax.numpy as jnp
from jax import lax
from jax.experimental import pallas as pl
from jax.experimental.pallas import tpu as pltpu
from jax.sharding import PartitionSpec as P

MESH = pl.DeviceIdType.MESH
F32, BF16 = jnp.float32, jnp.bfloat16
HIGHEST = lax.Precision.HIGHEST

ROWS, COLS, RANK = 192, 5120, 32
DP, MP, XS, YS = 32, 8, 4, 4
PARTS = 8
WIDE = COLS // PARTS
ROW_TILES = 8
STREAMS = ((0, 384), (384, 256))
GROUPS = ((0, 1), (2, 3), (4, 5), (6,), (7,))
ZS = DP // YS
FAR_Z = (4, 3, 5, 2, 6, 1, 7, 0)
FAR = (2, 1, 3, 0)
FAR_DP = sorted(
    ((dz, dy) for dz in range(ZS) for dy in range(YS) if dz or dy),
    key=lambda d: -min(d[0], ZS - d[0]) - min(d[1], YS - d[1]),
)


def split(value, parts):
    out = []
    for _ in range(parts):
        piece = value.astype(BF16)
        out.append(piece)
        value = value - piece.astype(F32)
    return out


def dot(a, b):
    return jnp.dot(a, b, preferred_element_type=F32)


def full_dot(a, b, dims=((1,), (0,))):
    return lax.dot_general(a, b, (dims, ((), ())), precision=HIGHEST, preferred_element_type=F32)


def inverse_cholesky(gram):
    row_id = lax.broadcasted_iota(jnp.int32, (RANK, 128), 0)
    lane_id = lax.broadcasted_iota(jnp.int32, (RANK, 128), 1)
    table = jnp.concatenate([gram, jnp.zeros((RANK, 128 - RANK), F32)], axis=1)
    table = table + jnp.where(lane_id == row_id + RANK, 1.0, 0.0)
    for j in range(RANK - 1):
        row = table[j : j + 1, :] / table[j : j + 1, j : j + 1]
        column = jnp.where(row_id > j, table[:, j : j + 1], 0.0)
        table = table - column * row
    pivots = jnp.sum(jnp.where(lane_id == row_id, table, 0.0), axis=1, keepdims=True)
    return table[:, RANK : 2 * RANK] / jnp.sqrt(pivots)


def pack(gram):
    return jnp.concatenate([gram[8 * s : 8 * s + 8, :] for s in range(4)], axis=1)


def unpack(tile):
    return jnp.concatenate([tile[:, 32 * s : 32 * s + 32] for s in range(4)], axis=0)


def stack_left(value):
    h, m, l = [p.astype(F32) for p in split(value, 3)]
    return jnp.concatenate([h, h, m, m, h, l], axis=0)


def stack_right(value):
    h, m, l = split(value, 3)
    return jnp.concatenate([h, m, h, m, l, h], axis=0)


def exchange(
    g_hbm, e_hbm, seed_hbm, both_ref, right_ref, wide_ref, left_ref,
    g_buf, e_buf, seed_buf, start, merged,
    left_tiles, left_in, left_all,
    gram_in, gram_in2,
    core_out_a, core_in_a, own_a, xy_in_a, z_in_a, full_a,
    core_out_b, core_in_b, own_b, xy_in_b, z_in_b, full_b,
    load_sem, seed_sem,
    lt_send, lt_recv, la_send, la_recv, gr_send, gr_recv,
    core_send, core_recv, xy_send, xy_recv, z_send, z_recv,
    ag_send, ag_recv, ac_send, ac_recv,
):
    me = lax.axis_index("dp")
    mp = lax.axis_index("mp")
    z, y = me // YS, me % YS
    x, core = mp // 2, mp % 2
    sibling = (me, x * 2 + 1 - core)

    def plane(kx, ky):
        return (z * YS + lax.rem(y + ky, YS), lax.rem(x + kx, XS) * 2 + core)

    def over_dp(dz, dy):
        return (lax.rem(z + dz, ZS) * YS + lax.rem(y + dy, YS), mp)

    barrier = pltpu.get_barrier_semaphore()
    seed_copy = pltpu.make_async_copy(seed_hbm, seed_buf, seed_sem)
    seed_copy.start()
    peers = [over_dp(*d) for d in FAR_DP] + [plane(kx, ky) for kx in FAR[:3] for ky in FAR[:3]]
    peers += [(me, lax.rem(mp + k, MP)) for k in range(1, MP)]
    for peer in peers:
        pl.semaphore_signal(barrier, inc=1, device_id=peer, device_id_type=MESH)

    loads = []
    for i in range(PARTS):
        columns = pl.ds(i * WIDE, WIDE)
        pair = (
            pltpu.make_async_copy(g_hbm.at[:, columns], g_buf.at[i], load_sem.at[0, i]),
            pltpu.make_async_copy(e_hbm.at[:, columns], e_buf.at[i], load_sem.at[1, i]),
        )
        for copy in pair:
            copy.start()
        loads.append(pair)

    seed_copy.wait()
    seeds = seed_buf[...].astype(F32) * (1.0 / 1024.0)
    less = seeds - seeds[0:1, :]
    shorter = jnp.sum(less * less, axis=1, keepdims=True) < jnp.sum(seeds * seeds, axis=1, keepdims=True)
    first = lax.broadcasted_iota(jnp.int32, (RANK, 1), 0) == 0
    take = jnp.where(jnp.logical_and(shorter, jnp.logical_not(first)), 1.0, 0.0)
    seeds = seeds - take * seeds[0:1, :]
    high, low = split(seeds, 2)
    blank = jnp.zeros((64, WIDE), BF16)
    for i in range(PARTS):
        columns = slice(i * WIDE, (i + 1) * WIDE)
        start[i] = jnp.concatenate([high[:, columns], low[:, columns], blank], axis=0)

    def product(group):
        a = jnp.concatenate([merged[i] for i in group], axis=1)
        b = jnp.concatenate([start[i] for i in group], axis=1)
        return lax.dot_general(a, b, (((1,), (1,)), ((), ())), preferred_element_type=F32)

    total = jnp.zeros((2 * ROWS, 128), F32)
    for n, group in enumerate(GROUPS):
        for i in group:
            for copy in loads[i]:
                copy.wait()
        for i in group:
            both = g_buf[i].astype(F32) + e_buf[i]
            both_ref[i] = both
            upper, lower = split(both, 2)
            merged[i, 0:ROWS, :] = upper
            merged[i, ROWS : 2 * ROWS, :] = lower
        if n:
            total = total + product(GROUPS[n - 1])
    total = total + product(GROUPS[-1])
    left = total[0:ROWS] + total[ROWS : 2 * ROWS]
    turned = jnp.transpose(jnp.concatenate([left, jnp.zeros((64, 128), F32)], axis=0))
    left = (turned[0:RANK] + turned[RANK : 2 * RANK]) * 1.024
    for t in range(2):
        for s in range(4):
            left_tiles[4 * t + s] = left[8 * s : 8 * s + 8, 128 * t : 128 * t + 128]

    pl.semaphore_wait(barrier, len(peers))

    def remote(src, dst, send, recv, device):
        return pltpu.make_async_remote_copy(
            src_ref=src, dst_ref=dst, send_sem=send, recv_sem=recv, device_id=device, device_id_type=MESH
        )

    def wait_bytes(ref, sem):
        pltpu.make_async_copy(ref, ref, sem).wait()

    left_owner = y == lax.rem(z, YS)

    for dz in FAR_Z:
        tile = lax.rem(z + dz, ROW_TILES)
        owner = tile * YS + lax.rem(tile, YS)

        @pl.when(owner != me)
        def _():
            remote(left_tiles.at[tile], left_in.at[me], lt_send, lt_recv, (owner, mp)).start()

    @pl.when(left_owner)
    def _():
        left_in[me] = left_tiles[z]
        wait_bytes(left_in.at[pl.ds(0, DP - 1)], lt_recv)
        left_all[z] = jnp.sum(left_in[...], axis=0)

        for d in FAR_DP:
            remote(left_all.at[z], left_all.at[z], la_send, la_recv, over_dp(*d)).start()

        wait_bytes(left_all.at[pl.ds(0, ROW_TILES - 1)], la_recv)

    @pl.when(jnp.logical_not(left_owner))
    def _():
        wait_bytes(left_all.at[pl.ds(0, ROW_TILES)], la_recv)

    left0 = jnp.concatenate(
        [jnp.concatenate([left_all[4 * t + s] for s in range(4)], axis=0) for t in range(2)], axis=1
    )

    def send_gram(slots, which, value):
        slots[mp] = pack(full_dot(value, value, ((1,), (1,))))

        @pl.loop(1, MP)
        def _(k):
            remote(
                slots.at[mp], slots.at[mp], gr_send.at[which], gr_recv.at[which], (me, lax.rem(mp + k, MP))
            ).start()

    def take_gram(slots, which):
        wait_bytes(slots.at[pl.ds(0, MP - 1)], gr_recv.at[which])
        return unpack(jnp.sum(slots[...], axis=0))

    send_gram(gram_in, 0, left0)

    pieces = jnp.concatenate([p.astype(F32) for p in split(left0[:, 0:ROWS], 3)], axis=0)
    pieces = jnp.concatenate([pieces, pieces], axis=1).astype(BF16)
    mine = core * XS + x
    streams = (
        (core_out_a, core_in_a, own_a, xy_in_a, z_in_a, full_a),
        (core_out_b, core_in_b, own_b, xy_in_b, z_in_b, full_b),
    )

    def right_part(into, part, columns):
        value = dot(pieces, merged[part, :, columns])
        value = value[0:32] + (value[32:64] + value[64:96])
        for s in range(YS):
            into[s] = value[8 * s : 8 * s + 8]

    def products(n):
        core_out, core_in, own = streams[n][0:3]
        columns = slice(STREAMS[n][0], sum(STREAMS[n]))
        for k in FAR:
            right_part(core_out.at[k], (1 - core) * XS + lax.rem(x + k, XS), columns)
            remote(core_out.at[k], core_in.at[k], core_send.at[n], core_recv.at[n, k], sibling).start()
        for k in FAR:
            right_part(own.at[k], core * XS + lax.rem(x + k, XS), columns)

    def send_plane(n):
        core_in, own, xy_in = streams[n][1:4]
        for kx in FAR:
            wait_bytes(core_in.at[kx], core_recv.at[n, kx])
            own[kx] = own[kx] + core_in[kx]
            for ky in FAR:
                if kx or ky:
                    remote(
                        own.at[kx, lax.rem(y + ky, YS)], xy_in.at[kx * YS + ky - 1],
                        xy_send.at[n], xy_recv.at[n], plane(kx, ky),
                    ).start()

    def send_z(n):
        own, xy_in, z_in = streams[n][2:5]
        wait_bytes(xy_in, xy_recv.at[n])
        z_in[z] = own[0, y] + jnp.sum(xy_in[...], axis=0)
        for dz in FAR_Z[:-1]:
            remote(z_in.at[z], z_in.at[z], z_send.at[n], z_recv.at[n], over_dp(dz, 0)).start()

    def gather_plane(n):
        z_in, full = streams[n][4:6]
        wait_bytes(z_in.at[pl.ds(0, ZS - 1)], z_recv.at[n])
        full[mine, y] = jnp.sum(z_in[...], axis=0)
        for kx in FAR:
            for ky in FAR:
                if kx or ky:
                    remote(
                        full.at[mine, y], full.at[mine, y], ag_send.at[n], ag_recv.at[n, kx], plane(kx, ky)
                    ).start()

    products(0)
    send_plane(0)
    products(1)
    send_plane(1)

    inverse1 = inverse_cholesky(take_gram(gram_in, 0))
    left1 = full_dot(inverse1, left0)
    send_gram(gram_in2, 1, left1)

    send_z(0)
    send_z(1)

    inverse2 = inverse_cholesky(take_gram(gram_in2, 1))
    left2 = full_dot(inverse2, left1)[:, 0:ROWS]
    left_ref[...] = left2
    wide_ref[...] = jnp.transpose(stack_left(left2)).astype(BF16)
    mix = full_dot(inverse2, inverse1)
    mix = jnp.transpose(jnp.pad(mix, ((0, 96), (0, 96))))[0:RANK]
    mix = jnp.transpose(stack_left(mix)).astype(BF16)[0:RANK]

    gather_plane(0)
    gather_plane(1)

    def right_of(n, part):
        columns = slice(STREAMS[n][0], sum(STREAMS[n]))
        sums = jnp.concatenate([streams[n][5][part, s] for s in range(4)], axis=0)
        right_ref[part, :, columns] = dot(mix, stack_right(sums)) * (1.0 / DP)

    near = (0, 1, 3, 2)
    for n in range(2):
        full = streams[n][5]
        for kx in near:
            got = core * XS + lax.rem(x + XS - kx, XS)
            wait_bytes(full.at[0, pl.ds(0, YS if kx else YS - 1)], ag_recv.at[n, kx])
            remote(full.at[got], full.at[got], ac_send.at[n], ac_recv.at[n, kx], sibling).start()
            right_of(n, got)
    for n in range(2):
        full = streams[n][5]
        for kx in near:
            wait_bytes(full.at[0], ac_recv.at[n, kx])
            right_of(n, (1 - core) * XS + lax.rem(x + XS - kx, XS))

    @pl.when(left_owner)
    def _():
        wait_bytes(left_in.at[pl.ds(0, ROW_TILES - 1)], lt_send)
        wait_bytes(left_in.at[pl.ds(0, DP - 1)], la_send)

    @pl.when(jnp.logical_not(left_owner))
    def _():
        wait_bytes(left_in.at[pl.ds(0, ROW_TILES)], lt_send)

    for which in range(2):
        wait_bytes(left_in.at[pl.ds(0, MP - 1)], gr_send.at[which])
    for n, (core_out, _, _, xy_in, z_in, _) in enumerate(streams):
        wait_bytes(core_out, core_send.at[n])
        wait_bytes(xy_in, xy_send.at[n])
        wait_bytes(z_in.at[pl.ds(0, ZS - 1)], z_send.at[n])
        wait_bytes(xy_in, ag_send.at[n])
        wait_bytes(core_out, ac_send.at[n])


def run_exchange(gradients, errors, seeds):
    hbm = pl.BlockSpec(memory_space=pltpu.HBM)
    vmem = pl.BlockSpec(memory_space=pltpu.VMEM)
    dma = pltpu.SemaphoreType.DMA
    return pl.pallas_call(
        exchange,
        out_shape=(
            jax.ShapeDtypeStruct((PARTS, ROWS, WIDE), F32),
            jax.ShapeDtypeStruct((PARTS, RANK, WIDE), F32),
            jax.ShapeDtypeStruct((ROWS, 6 * RANK), BF16),
            jax.ShapeDtypeStruct((RANK, ROWS), F32),
        ),
        in_specs=[hbm, hbm, hbm],
        out_specs=(vmem,) * 4,
        scratch_shapes=[
            pltpu.VMEM((PARTS, ROWS, WIDE), BF16),
            pltpu.VMEM((PARTS, ROWS, WIDE), F32),
            pltpu.VMEM((RANK, COLS), jnp.int32),
            pltpu.VMEM((PARTS, 128, WIDE), BF16),
            pltpu.VMEM((PARTS, 2 * ROWS, WIDE), BF16),
            pltpu.VMEM((ROW_TILES, 8, 128), F32),
            pltpu.VMEM((DP, 8, 128), F32),
            pltpu.VMEM((ROW_TILES, 8, 128), F32),
            pltpu.VMEM((MP, 8, 128), F32),
            pltpu.VMEM((MP, 8, 128), F32),
            *(
                pltpu.VMEM(shape + (8, width), F32)
                for _, width in STREAMS
                for shape in ((XS, YS), (XS, YS), (XS, YS), (XS * YS - 1,), (ZS,), (PARTS, YS))
            ),
            dma((2, PARTS)),
            dma,
            dma, dma, dma, dma, dma((2,)), dma((2,)),
            dma((2,)), dma((2, XS)), dma((2,)), dma((2,)), dma((2,)), dma((2,)),
            dma((2,)), dma((2, XS)), dma((2,)), dma((2, XS)),
        ],
        compiler_params=pltpu.CompilerParams(
            collective_id=0, has_side_effects=True, vmem_limit_bytes=40 * 1024 * 1024
        ),
        cost_estimate=pl.CostEstimate(flops=10**9, bytes_accessed=8 * 10**6, transcendentals=0),
        name="exchange",
    )(*(pltpu.with_memory_space_constraint(v, pltpu.HBM) for v in (gradients, errors, seeds)))


def finish(
    both_ref, right_ref, wide_ref, left_ref, new_hbm, update_hbm, right_hbm, left_hbm,
    new_buf, update_buf, new_sem, update_sem, right_sem, left_sem,
):
    copies = [pltpu.make_async_copy(left_ref, left_hbm, left_sem)]
    copies[0].start()
    for part in range(PARTS):
        columns = pl.ds(part * WIDE, WIDE)
        approx = dot(wide_ref[...], stack_right(right_ref[part]))
        new_buf[part] = both_ref[part] - approx
        update_buf[part] = approx.astype(BF16)
        for copy in (
            pltpu.make_async_copy(new_buf.at[part], new_hbm.at[:, columns], new_sem.at[part]),
            pltpu.make_async_copy(update_buf.at[part], update_hbm.at[:, columns], update_sem.at[part]),
            pltpu.make_async_copy(right_ref.at[part], right_hbm.at[:, columns], right_sem.at[part]),
        ):
            copy.start()
            copies.append(copy)
    for copy in copies:
        copy.wait()


def run_finish(*operands):
    hbm = pl.BlockSpec(memory_space=pltpu.HBM)
    vmem = pl.BlockSpec(memory_space=pltpu.VMEM)
    dma = pltpu.SemaphoreType.DMA
    return pl.pallas_call(
        finish,
        out_shape=(
            jax.ShapeDtypeStruct((ROWS, COLS), F32),
            jax.ShapeDtypeStruct((ROWS, COLS), BF16),
            jax.ShapeDtypeStruct((RANK, COLS), F32),
            jax.ShapeDtypeStruct((RANK, ROWS), F32),
        ),
        in_specs=[vmem] * 4,
        out_specs=(hbm,) * 4,
        scratch_shapes=[
            pltpu.VMEM((PARTS, ROWS, WIDE), F32),
            pltpu.VMEM((PARTS, ROWS, WIDE), BF16),
            dma((PARTS,)), dma((PARTS,)), dma((PARTS,)), dma,
        ],
        compiler_params=pltpu.CompilerParams(vmem_limit_bytes=40 * 1024 * 1024),
        cost_estimate=pl.CostEstimate(flops=10**9, bytes_accessed=10**7, transcendentals=0),
        name="finish",
    )(*operands)


def local(gradients, errors, seed_table):
    new_errors, update, right, left = run_finish(*run_exchange(gradients[0], errors[0], seed_table.T))
    return (new_errors[None], update, right.T, left.T)


def solution(mesh):
    in_specs = (P("dp", "mp", None), P("dp", "mp", None), P())
    out_specs = (P("dp", "mp", None), P("mp", None), P(), P("mp", None))
    return jax.shard_map(local, mesh=mesh, in_specs=in_specs, out_specs=out_specs, check_vma=False)
```

```python
import jax
import jax.numpy as jnp
from jax import lax
from jax.experimental import pallas as pl
from jax.experimental.pallas import tpu as pltpu
from jax.sharding import PartitionSpec as P

MESH = pl.DeviceIdType.MESH
F32, BF16 = jnp.float32, jnp.bfloat16
HIGHEST = lax.Precision.HIGHEST

ROWS, COLS, RANK = 192, 5120, 32
DP, MP, XS, YS = 32, 8, 4, 4
PARTS = 8
WIDE = COLS // PARTS
ROW_TILES = 6
STREAMS = ((0, 384), (384, 256))
GROUPS = ((0, 1), (2, 3), (4, 5), (6,), (7,))
ZS = DP // YS
FAR_Z = (4, 3, 5, 2, 6, 1, 7, 0)
FAR = (2, 1, 3, 0)
LAG = 2


def split(value, parts):
    out = []
    for _ in range(parts):
        piece = value.astype(BF16)
        out.append(piece)
        value = value - piece.astype(F32)
    return out


def dot(a, b):
    return jnp.dot(a, b, preferred_element_type=F32)


def full_dot(a, b, dims=((1,), (0,))):
    return lax.dot_general(a, b, (dims, ((), ())), precision=HIGHEST, preferred_element_type=F32)


def inverse_cholesky(gram):
    row_id = lax.broadcasted_iota(jnp.int32, (RANK, 128), 0)
    lane_id = lax.broadcasted_iota(jnp.int32, (RANK, 128), 1)
    table = jnp.concatenate([gram, jnp.zeros((RANK, 128 - RANK), F32)], axis=1)
    table = table + jnp.where(lane_id == row_id + RANK, 1.0, 0.0)
    for j in range(RANK - 1):
        row = table[j : j + 1, :] / table[j : j + 1, j : j + 1]
        column = jnp.where(row_id > j, table[:, j : j + 1], 0.0)
        table = table - column * row
    pivots = jnp.sum(jnp.where(lane_id == row_id, table, 0.0), axis=1, keepdims=True)
    return table[:, RANK : 2 * RANK] / jnp.sqrt(pivots)


def pack(gram):
    return jnp.concatenate([gram[8 * s : 8 * s + 8, :] for s in range(4)], axis=1)


def unpack(tile):
    return jnp.concatenate([tile[:, 32 * s : 32 * s + 32] for s in range(4)], axis=0)


def stack_left(value):
    h, m, l = [p.astype(F32) for p in split(value, 3)]
    return jnp.concatenate([h, h, m, m, h, l], axis=0)


def stack_right(value):
    h, m, l = split(value, 3)
    return jnp.concatenate([h, m, h, m, l, h], axis=0)


def exchange(
    g_hbm, e_hbm, seed_hbm, both_ref, right_ref, wide_ref, left_ref,
    g_buf, e_buf, seed_buf, start, merged,
    left_y, left_z,
    gram_in, gram_in2,
    core_out_a, core_in_a, own_a, xy_in_a, z_in_a, full_a,
    core_out_b, core_in_b, own_b, xy_in_b, z_in_b, full_b,
    load_sem, seed_sem,
    ly_send, ly_recv, lz_send, lz_recv, gr_send, gr_recv,
    core_send, core_recv, xy_send, xy_recv, z_send, z_recv,
    ag_send, ag_recv, ac_send, ac_recv,
):
    me = lax.axis_index("dp")
    mp = lax.axis_index("mp")
    z, y = me // YS, me % YS
    x, core = mp // 2, mp % 2
    sibling = (me, x * 2 + 1 - core)

    def plane(kx, ky):
        return (z * YS + lax.rem(y + ky, YS), lax.rem(x + kx, XS) * 2 + core)

    def over_dp(dz, dy):
        return (lax.rem(z + dz, ZS) * YS + lax.rem(y + dy, YS), mp)

    barrier = pltpu.get_barrier_semaphore()
    seed_copy = pltpu.make_async_copy(seed_hbm, seed_buf, seed_sem)
    seed_copy.start()
    peers = [over_dp(dz, 0) for dz in FAR_Z[:-1]] + [plane(kx, ky) for kx in FAR[:3] for ky in FAR[:3]]
    peers += [over_dp(0, dy) for dy in FAR[:3]] + [(me, lax.rem(mp + k, MP)) for k in range(1, MP)]
    for peer in peers:
        pl.semaphore_signal(barrier, inc=1, device_id=peer, device_id_type=MESH)

    loads = []
    for i in range(PARTS):
        columns = pl.ds(i * WIDE, WIDE)
        pair = (
            pltpu.make_async_copy(g_hbm.at[:, columns], g_buf.at[i], load_sem.at[0, i]),
            pltpu.make_async_copy(e_hbm.at[:, columns], e_buf.at[i], load_sem.at[1, i]),
        )
        for copy in pair:
            copy.start()
        loads.append(pair)

    seed_copy.wait()
    seeds = seed_buf[...].astype(F32) * (1.0 / 1024.0)
    less = seeds - seeds[0:1, :]
    shorter = jnp.sum(less * less, axis=1, keepdims=True) < jnp.sum(seeds * seeds, axis=1, keepdims=True)
    first = lax.broadcasted_iota(jnp.int32, (RANK, 1), 0) == 0
    take = jnp.where(jnp.logical_and(shorter, jnp.logical_not(first)), 1.0, 0.0)
    seeds = seeds - take * seeds[0:1, :]
    high, low = split(seeds, 2)
    for i in range(PARTS):
        columns = slice(i * WIDE, (i + 1) * WIDE)
        start[i] = jnp.concatenate([high[:, columns], low[:, columns]], axis=0)

    def product(group):
        a = jnp.concatenate([merged[i] for i in group], axis=1)
        b = jnp.concatenate([start[i] for i in group], axis=1)
        return lax.dot_general(a, b, (((1,), (1,)), ((), ())), preferred_element_type=F32)

    total = jnp.zeros((2 * ROWS, 64), F32)
    for n, group in enumerate(GROUPS):
        for i in group:
            for copy in loads[i]:
                copy.wait()
        for i in group:
            both = g_buf[i].astype(F32) + e_buf[i]
            both_ref[i] = both
            upper, lower = split(both, 2)
            merged[i, 0:ROWS, :] = upper
            merged[i, ROWS : 2 * ROWS, :] = lower
        if n:
            total = total + product(GROUPS[n - 1])
    total = total + product(GROUPS[-1])
    left = total[0:ROWS] + total[ROWS : 2 * ROWS]
    turned = jnp.transpose(jnp.pad(left, ((0, 64), (0, 64))))
    left = (turned[0:RANK] + turned[RANK : 2 * RANK]) * 1.024
    for s in range(4):
        left_y[y, s] = left[8 * s : 8 * s + 8, 0:128]
    for s in range(2):
        rest = left[16 * s : 16 * s + 16, 128:256]
        left_y[y, 4 + s] = rest[0:8] + pltpu.roll(rest[8:16], 64, 1)

    pl.semaphore_wait(barrier, len(peers))

    def remote(src, dst, send, recv, device):
        return pltpu.make_async_remote_copy(
            src_ref=src, dst_ref=dst, send_sem=send, recv_sem=recv, device_id=device, device_id_type=MESH
        )

    def wait_bytes(ref, sem):
        pltpu.make_async_copy(ref, ref, sem).wait()

    for dy in FAR[:3]:
        remote(left_y.at[y], left_y.at[y], ly_send, ly_recv, over_dp(0, dy)).start()
    wait_bytes(left_y.at[pl.ds(0, YS - 1)], ly_recv)
    left_z[z] = jnp.sum(left_y[...], axis=0)
    for dz in FAR_Z[:-1]:
        remote(left_z.at[z], left_z.at[z], lz_send, lz_recv, over_dp(dz, 0)).start()
    wait_bytes(left_z.at[pl.ds(0, ZS - 1)], lz_recv)
    left = jnp.sum(left_z[...], axis=0)
    half = lax.broadcasted_iota(jnp.int32, (8, 128), 1) < 64
    rest = [jnp.where(half, v, 0.0) for t in (4, 5) for v in (left[t], pltpu.roll(left[t], 64, 1))]
    left0 = jnp.concatenate(
        [jnp.concatenate([left[s] for s in range(4)], axis=0), jnp.concatenate(rest, axis=0)], axis=1
    )

    def send_gram(slots, which, value):
        slots[mp] = pack(full_dot(value, value, ((1,), (1,))))

        @pl.loop(1, MP)
        def _(k):
            remote(
                slots.at[mp], slots.at[mp], gr_send.at[which], gr_recv.at[which], (me, lax.rem(mp + k, MP))
            ).start()

    def take_gram(slots, which):
        wait_bytes(slots.at[pl.ds(0, MP - 1)], gr_recv.at[which])
        return unpack(jnp.sum(slots[...], axis=0))

    send_gram(gram_in, 0, left0)

    pieces = jnp.concatenate([p.astype(F32) for p in split(left0[:, 0:ROWS], 3)], axis=0)
    pieces = jnp.concatenate([pieces, pieces], axis=1).astype(BF16)
    mine = core * XS + x
    streams = (
        (core_out_a, core_in_a, own_a, xy_in_a, z_in_a, full_a),
        (core_out_b, core_in_b, own_b, xy_in_b, z_in_b, full_b),
    )

    def right_part(into, part, columns):
        value = dot(pieces, merged[part, :, columns])
        value = value[0:32] + (value[32:64] + value[64:96])
        for s in range(YS):
            into[s] = value[8 * s : 8 * s + 8]

    def products(n, k):
        core_out, core_in, own = streams[n][0:3]
        columns = slice(STREAMS[n][0], sum(STREAMS[n]))
        right_part(core_out.at[k], (1 - core) * XS + lax.rem(x + k, XS), columns)
        remote(core_out.at[k], core_in.at[k], core_send.at[n], core_recv.at[n, k], sibling).start()
        right_part(own.at[k], core * XS + lax.rem(x + k, XS), columns)

    def send_plane(n, kx):
        core_in, own, xy_in = streams[n][1:4]
        wait_bytes(core_in.at[kx], core_recv.at[n, kx])
        own[kx] = own[kx] + core_in[kx]
        for ky in FAR:
            if kx or ky:
                remote(
                    own.at[kx, lax.rem(y + ky, YS)], xy_in.at[kx * YS + ky - 1],
                    xy_send.at[n], xy_recv.at[n], plane(kx, ky),
                ).start()

    def send_z(n):
        own, xy_in, z_in = streams[n][2:5]
        wait_bytes(xy_in, xy_recv.at[n])
        z_in[z] = own[0, y] + jnp.sum(xy_in[...], axis=0)
        for dz in FAR_Z[:-1]:
            remote(z_in.at[z], z_in.at[z], z_send.at[n], z_recv.at[n], over_dp(dz, 0)).start()

    def gather_plane(n):
        z_in, full = streams[n][4:6]
        wait_bytes(z_in.at[pl.ds(0, ZS - 1)], z_recv.at[n])
        full[mine, y] = jnp.sum(z_in[...], axis=0)
        for kx in FAR:
            for ky in FAR:
                if kx or ky:
                    remote(
                        full.at[mine, y], full.at[mine, y], ag_send.at[n], ag_recv.at[n, kx], plane(kx, ky)
                    ).start()

    chunks = [(n, k) for n in range(2) for k in FAR]
    for i, chunk in enumerate(chunks):
        products(*chunk)
        if i >= LAG:
            send_plane(*chunks[i - LAG])
    for chunk in chunks[-LAG:]:
        send_plane(*chunk)

    send_z(0)
    send_z(1)

    inverse1 = inverse_cholesky(take_gram(gram_in, 0))
    left1 = full_dot(inverse1, left0)
    send_gram(gram_in2, 1, left1)

    gather_plane(0)
    gather_plane(1)

    inverse2 = inverse_cholesky(take_gram(gram_in2, 1))
    left2 = full_dot(inverse2, left1)[:, 0:ROWS]
    left_ref[...] = left2
    wide_ref[...] = jnp.transpose(stack_left(left2)).astype(BF16)
    mix = full_dot(inverse2, inverse1)
    mix = jnp.transpose(jnp.pad(mix, ((0, 96), (0, 96))))[0:RANK]
    mix = jnp.transpose(stack_left(mix)).astype(BF16)[0:RANK]

    def right_of(n, part):
        columns = slice(STREAMS[n][0], sum(STREAMS[n]))
        sums = jnp.concatenate([streams[n][5][part, s] for s in range(4)], axis=0)
        right_ref[part, :, columns] = dot(mix, stack_right(sums)) * (1.0 / DP)

    near = (0, 1, 3, 2)
    for n in range(2):
        full = streams[n][5]
        for kx in near:
            got = core * XS + lax.rem(x + XS - kx, XS)
            wait_bytes(full.at[0, pl.ds(0, YS if kx else YS - 1)], ag_recv.at[n, kx])
            remote(full.at[got], full.at[got], ac_send.at[n], ac_recv.at[n, kx], sibling).start()
            right_of(n, got)
    for n in range(2):
        full = streams[n][5]
        for kx in near:
            wait_bytes(full.at[0], ac_recv.at[n, kx])
            right_of(n, (1 - core) * XS + lax.rem(x + XS - kx, XS))

    wait_bytes(left_y.at[pl.ds(0, YS - 1)], ly_send)
    wait_bytes(left_z.at[pl.ds(0, ZS - 1)], lz_send)
    for which in range(2):
        wait_bytes(gram_in.at[pl.ds(0, MP - 1)], gr_send.at[which])
    for n, (core_out, _, _, xy_in, z_in, _) in enumerate(streams):
        wait_bytes(core_out, core_send.at[n])
        wait_bytes(xy_in, xy_send.at[n])
        wait_bytes(z_in.at[pl.ds(0, ZS - 1)], z_send.at[n])
        wait_bytes(xy_in, ag_send.at[n])
        wait_bytes(core_out, ac_send.at[n])


def run_exchange(gradients, errors, seeds):
    hbm = pl.BlockSpec(memory_space=pltpu.HBM)
    vmem = pl.BlockSpec(memory_space=pltpu.VMEM)
    dma = pltpu.SemaphoreType.DMA
    return pl.pallas_call(
        exchange,
        out_shape=(
            jax.ShapeDtypeStruct((PARTS, ROWS, WIDE), F32),
            jax.ShapeDtypeStruct((PARTS, RANK, WIDE), F32),
            jax.ShapeDtypeStruct((ROWS, 6 * RANK), BF16),
            jax.ShapeDtypeStruct((RANK, ROWS), F32),
        ),
        in_specs=[hbm, hbm, hbm],
        out_specs=(vmem,) * 4,
        scratch_shapes=[
            pltpu.VMEM((PARTS, ROWS, WIDE), BF16),
            pltpu.VMEM((PARTS, ROWS, WIDE), F32),
            pltpu.VMEM((RANK, COLS), jnp.int32),
            pltpu.VMEM((PARTS, 64, WIDE), BF16),
            pltpu.VMEM((PARTS, 2 * ROWS, WIDE), BF16),
            pltpu.VMEM((YS, ROW_TILES, 8, 128), F32),
            pltpu.VMEM((ZS, ROW_TILES, 8, 128), F32),
            pltpu.VMEM((MP, 8, 128), F32),
            pltpu.VMEM((MP, 8, 128), F32),
            *(
                pltpu.VMEM(shape + (8, width), F32)
                for _, width in STREAMS
                for shape in ((XS, YS), (XS, YS), (XS, YS), (XS * YS - 1,), (ZS,), (PARTS, YS))
            ),
            dma((2, PARTS)),
            dma,
            dma, dma, dma, dma, dma((2,)), dma((2,)),
            dma((2,)), dma((2, XS)), dma((2,)), dma((2,)), dma((2,)), dma((2,)),
            dma((2,)), dma((2, XS)), dma((2,)), dma((2, XS)),
        ],
        compiler_params=pltpu.CompilerParams(
            collective_id=0, has_side_effects=True, vmem_limit_bytes=40 * 1024 * 1024
        ),
        cost_estimate=pl.CostEstimate(flops=10**9, bytes_accessed=8 * 10**6, transcendentals=0),
        name="exchange",
    )(*(pltpu.with_memory_space_constraint(v, pltpu.HBM) for v in (gradients, errors, seeds)))


def finish(
    both_ref, right_ref, wide_ref, left_ref, new_hbm, update_hbm, right_hbm, left_hbm,
    new_buf, update_buf, new_sem, update_sem, right_sem, left_sem,
):
    copies = [pltpu.make_async_copy(left_ref, left_hbm, left_sem)]
    copies[0].start()
    for part in range(PARTS):
        columns = pl.ds(part * WIDE, WIDE)
        approx = dot(wide_ref[...], stack_right(right_ref[part]))
        new_buf[part] = both_ref[part] - approx
        update_buf[part] = approx.astype(BF16)
        for copy in (
            pltpu.make_async_copy(new_buf.at[part], new_hbm.at[:, columns], new_sem.at[part]),
            pltpu.make_async_copy(update_buf.at[part], update_hbm.at[:, columns], update_sem.at[part]),
            pltpu.make_async_copy(right_ref.at[part], right_hbm.at[:, columns], right_sem.at[part]),
        ):
            copy.start()
            copies.append(copy)
    for copy in copies:
        copy.wait()


def run_finish(*operands):
    hbm = pl.BlockSpec(memory_space=pltpu.HBM)
    vmem = pl.BlockSpec(memory_space=pltpu.VMEM)
    dma = pltpu.SemaphoreType.DMA
    return pl.pallas_call(
        finish,
        out_shape=(
            jax.ShapeDtypeStruct((ROWS, COLS), F32),
            jax.ShapeDtypeStruct((ROWS, COLS), BF16),
            jax.ShapeDtypeStruct((RANK, COLS), F32),
            jax.ShapeDtypeStruct((RANK, ROWS), F32),
        ),
        in_specs=[vmem] * 4,
        out_specs=(hbm,) * 4,
        scratch_shapes=[
            pltpu.VMEM((PARTS, ROWS, WIDE), F32),
            pltpu.VMEM((PARTS, ROWS, WIDE), BF16),
            dma((PARTS,)), dma((PARTS,)), dma((PARTS,)), dma,
        ],
        compiler_params=pltpu.CompilerParams(vmem_limit_bytes=40 * 1024 * 1024),
        cost_estimate=pl.CostEstimate(flops=10**9, bytes_accessed=10**7, transcendentals=0),
        name="finish",
    )(*operands)


def local(gradients, errors, seed_table):
    new_errors, update, right, left = run_finish(*run_exchange(gradients[0], errors[0], seed_table.T))
    return (new_errors[None], update, right.T, left.T)


def solution(mesh):
    in_specs = (P("dp", "mp", None), P("dp", "mp", None), P())
    out_specs = (P("dp", "mp", None), P("mp", None), P(), P("mp", None))
    return jax.shard_map(local, mesh=mesh, in_specs=in_specs, out_specs=out_specs, check_vma=False)
```

```python
import jax
import jax.numpy as jnp
from jax import lax
from jax.experimental import pallas as pl
from jax.experimental.pallas import tpu as pltpu
from jax.sharding import PartitionSpec as P

MESH = pl.DeviceIdType.MESH
F32, BF16 = jnp.float32, jnp.bfloat16
HIGHEST = lax.Precision.HIGHEST

ROWS, COLS, RANK = 192, 5120, 32
DP, MP, XS, YS = 32, 8, 4, 4
PARTS = 8
WIDE = COLS // PARTS
ROW_TILES = 6
STREAMS = ((0, 384), (384, 256))
GROUPS = ((0, 1), (2, 3), (4, 5), (6,), (7,))
ZS = DP // YS
FAR_Z = (4, 3, 5, 2, 6, 1, 7, 0)
FAR = (2, 1, 3, 0)


def split(value, parts):
    out = []
    for _ in range(parts):
        piece = value.astype(BF16)
        out.append(piece)
        value = value - piece.astype(F32)
    return out


def dot(a, b):
    return jnp.dot(a, b, preferred_element_type=F32)


def full_dot(a, b, dims=((1,), (0,))):
    return lax.dot_general(a, b, (dims, ((), ())), precision=HIGHEST, preferred_element_type=F32)


def inverse_cholesky(gram):
    row_id = lax.broadcasted_iota(jnp.int32, (RANK, 128), 0)
    lane_id = lax.broadcasted_iota(jnp.int32, (RANK, 128), 1)
    table = jnp.concatenate([gram, jnp.zeros((RANK, 128 - RANK), F32)], axis=1)
    table = table + jnp.where(lane_id == row_id + RANK, 1.0, 0.0)
    blocks = [table[8 * i : 8 * i + 8] for i in range(4)]
    for j in range(RANK - 1):
        at, within = j // 8, j % 8
        columns = {i: jnp.broadcast_to(blocks[i][:, j : j + 1], (8, 128)) for i in range(at, 4)}
        row = blocks[at][within : within + 1] * (1.0 / columns[at][within : within + 1])
        columns[at] = jnp.where(row_id[0:8] > within, columns[at], 0.0)
        for i, column in columns.items():
            blocks[i] = blocks[i] - column * row
    table = jnp.concatenate(blocks, axis=0)
    pivots = jnp.sum(jnp.where(lane_id == row_id, table, 0.0), axis=1, keepdims=True)
    return table[:, RANK : 2 * RANK] / jnp.sqrt(pivots)


def pack(gram):
    return jnp.concatenate([gram[8 * s : 8 * s + 8, :] for s in range(4)], axis=1)


def unpack(tile):
    return jnp.concatenate([tile[:, 32 * s : 32 * s + 32] for s in range(4)], axis=0)


def stack_left(value):
    h, m, l = [p.astype(F32) for p in split(value, 3)]
    return jnp.concatenate([h, h, m, m, h, l], axis=0)


def stack_right(value):
    h, m, l = split(value, 3)
    return jnp.concatenate([h, m, h, m, l, h], axis=0)


def exchange(
    g_hbm, e_hbm, seed_hbm, both_ref, right_ref, wide_ref, left_ref,
    g_buf, e_buf, seed_buf, start, merged,
    left_y, left_z, left_mine, left_other, other, other_split,
    gram_in, gram_in2,
    own_a, xy_in_a, z_in_a, full_a,
    own_b, xy_in_b, z_in_b, full_b,
    load_sem, seed_sem,
    ly_send, ly_recv, lz_send, lz_recv, gr_send, gr_recv,
    lc_send, lc_recv, oc_send, oc_recv, xy_send, xy_recv, z_send, z_recv,
    ag_send, ag_recv, ac_send, ac_recv,
):
    me = lax.axis_index("dp")
    mp = lax.axis_index("mp")
    z, y = me // YS, me % YS
    x, core = mp // 2, mp % 2
    sibling = (me, x * 2 + 1 - core)

    def plane(kx, ky):
        return (z * YS + lax.rem(y + ky, YS), lax.rem(x + kx, XS) * 2 + core)

    def over_dp(dz, dy):
        return (lax.rem(z + dz, ZS) * YS + lax.rem(y + dy, YS), mp)

    barrier = pltpu.get_barrier_semaphore()
    seed_copy = pltpu.make_async_copy(seed_hbm, seed_buf, seed_sem)
    seed_copy.start()
    peers = [over_dp(dz, 0) for dz in FAR_Z[:-1]] + [plane(kx, ky) for kx in FAR[:3] for ky in FAR[:3]]
    peers += [over_dp(0, dy) for dy in FAR[:3]] + [(me, lax.rem(mp + k, MP)) for k in range(1, MP)]
    for peer in peers:
        pl.semaphore_signal(barrier, inc=1, device_id=peer, device_id_type=MESH)

    loads = []
    for i in range(PARTS):
        columns = pl.ds(i * WIDE, WIDE)
        pair = (
            pltpu.make_async_copy(g_hbm.at[:, columns], g_buf.at[i], load_sem.at[0, i]),
            pltpu.make_async_copy(e_hbm.at[:, columns], e_buf.at[i], load_sem.at[1, i]),
        )
        for copy in pair:
            copy.start()
        loads.append(pair)

    seed_copy.wait()
    seeds = seed_buf[...].astype(F32) * (1.0 / 1024.0)
    less = seeds - seeds[0:1, :]
    shorter = jnp.sum(less * less, axis=1, keepdims=True) < jnp.sum(seeds * seeds, axis=1, keepdims=True)
    first = lax.broadcasted_iota(jnp.int32, (RANK, 1), 0) == 0
    take = jnp.where(jnp.logical_and(shorter, jnp.logical_not(first)), 1.0, 0.0)
    seeds = seeds - take * seeds[0:1, :]
    high, low = split(seeds, 2)
    for i in range(PARTS):
        columns = slice(i * WIDE, (i + 1) * WIDE)
        start[i] = jnp.concatenate([high[:, columns], low[:, columns]], axis=0)

    def product(group):
        a = jnp.concatenate([merged[i] for i in group], axis=1)
        b = jnp.concatenate([start[i] for i in group], axis=1)
        return lax.dot_general(a, b, (((1,), (1,)), ((), ())), preferred_element_type=F32)

    total = jnp.zeros((2 * ROWS, 64), F32)
    for n, group in enumerate(GROUPS):
        for i in group:
            for copy in loads[i]:
                copy.wait()
        for i in group:
            both = g_buf[i].astype(F32) + e_buf[i]
            both_ref[i] = both
            upper, lower = split(both, 2)
            merged[i, 0:ROWS, :] = upper
            merged[i, ROWS : 2 * ROWS, :] = lower
        if n:
            total = total + product(GROUPS[n - 1])
    total = total + product(GROUPS[-1])
    left = total[0:ROWS] + total[ROWS : 2 * ROWS]
    turned = jnp.transpose(jnp.pad(left, ((0, 64), (0, 64))))
    left = (turned[0:RANK] + turned[RANK : 2 * RANK]) * 1.024
    for s in range(4):
        left_y[y, s] = left[8 * s : 8 * s + 8, 0:128]
    for s in range(2):
        rest = left[16 * s : 16 * s + 16, 128:256]
        left_y[y, 4 + s] = rest[0:8] + pltpu.roll(rest[8:16], 64, 1)

    pl.semaphore_wait(barrier, len(peers))

    def remote(src, dst, send, recv, device):
        return pltpu.make_async_remote_copy(
            src_ref=src, dst_ref=dst, send_sem=send, recv_sem=recv, device_id=device, device_id_type=MESH
        )

    def wait_bytes(ref, sem):
        pltpu.make_async_copy(ref, ref, sem).wait()

    for dy in FAR[:3]:
        remote(left_y.at[y], left_y.at[y], ly_send, ly_recv, over_dp(0, dy)).start()
    for k in FAR:
        part = (1 - core) * XS + lax.rem(x + k, XS)
        remote(both_ref.at[part], other.at[k], oc_send, oc_recv, sibling).start()
    wait_bytes(left_y.at[pl.ds(0, YS - 1)], ly_recv)
    left_z[z] = jnp.sum(left_y[...], axis=0)
    for dz in FAR_Z[:-1]:
        remote(left_z.at[z], left_z.at[z], lz_send, lz_recv, over_dp(dz, 0)).start()
    wait_bytes(other, oc_recv)
    for k in range(XS):
        upper, lower = split(other[k], 2)
        other_split[k, 0:ROWS, :] = upper
        other_split[k, ROWS : 2 * ROWS, :] = lower
    wait_bytes(left_z.at[pl.ds(0, ZS - 1)], lz_recv)
    left_mine[...] = jnp.sum(left_z[...], axis=0)
    remote(left_mine, left_other, lc_send, lc_recv, sibling).start()
    half = lax.broadcasted_iota(jnp.int32, (8, 128), 1) < 64

    def matrix(tiles):
        rest = [jnp.where(half, v, 0.0) for t in (4, 5) for v in (tiles[t], pltpu.roll(tiles[t], 64, 1))]
        return jnp.concatenate(
            [jnp.concatenate([tiles[s] for s in range(4)], axis=0), jnp.concatenate(rest, axis=0)], axis=1
        )

    left0 = matrix(left_mine)

    def send_gram(slots, which, value):
        slots[mp] = pack(full_dot(value, value, ((1,), (1,))))

        @pl.loop(1, MP)
        def _(k):
            remote(
                slots.at[mp], slots.at[mp], gr_send.at[which], gr_recv.at[which], (me, lax.rem(mp + k, MP))
            ).start()

    def take_gram(slots, which):
        wait_bytes(slots.at[pl.ds(0, MP - 1)], gr_recv.at[which])
        return unpack(jnp.sum(slots[...], axis=0))

    send_gram(gram_in, 0, left0)

    def pieces_of(left):
        rows = jnp.concatenate([p.astype(F32) for p in split(left[:, 0:ROWS], 3)], axis=0)
        return jnp.concatenate([rows, rows], axis=1).astype(BF16)

    pieces = pieces_of(left0)
    mine = core * XS + x
    streams = (
        (own_a, xy_in_a, z_in_a, full_a),
        (own_b, xy_in_b, z_in_b, full_b),
    )

    def right_part(rows, values, n):
        value = dot(rows, values[:, STREAMS[n][0] : sum(STREAMS[n])])
        return value[0:32] + (value[32:64] + value[64:96])

    def put(into, value, more):
        for s in range(YS):
            piece = value[8 * s : 8 * s + 8]
            into[s] = into[s] + piece if more else piece

    def my_rows(n, k):
        return right_part(pieces, merged.at[core * XS + lax.rem(x + k, XS)], n)

    def send_plane(n, kx):
        own, xy_in = streams[n][0:2]
        for ky in FAR:
            if kx or ky:
                remote(
                    own.at[kx, lax.rem(y + ky, YS)], xy_in.at[kx * YS + ky - 1],
                    xy_send.at[n], xy_recv.at[n], plane(kx, ky),
                ).start()

    def send_z(n):
        own, xy_in, z_in = streams[n][0:3]
        wait_bytes(xy_in, xy_recv.at[n])
        z_in[z] = own[0, y] + jnp.sum(xy_in[...], axis=0)
        for dz in FAR_Z[:-1]:
            remote(z_in.at[z], z_in.at[z], z_send.at[n], z_recv.at[n], over_dp(dz, 0)).start()

    def gather_plane(n):
        z_in, full = streams[n][2:4]
        wait_bytes(z_in.at[pl.ds(0, ZS - 1)], z_recv.at[n])
        full[mine, y] = jnp.sum(z_in[...], axis=0)
        for kx in FAR:
            for ky in FAR:
                if kx or ky:
                    remote(
                        full.at[mine, y], full.at[mine, y], ag_send.at[n], ag_recv.at[n, kx], plane(kx, ky)
                    ).start()

    for k in FAR:
        put(own_a.at[k], my_rows(0, k), False)
    wait_bytes(left_other, lc_recv)
    pieces_other = pieces_of(matrix(left_other))
    for n in range(2):
        for k in FAR:
            value = right_part(pieces_other, other_split.at[k], n)
            if n:
                value = value + my_rows(n, k)
            put(streams[n][0].at[k], value, n == 0)
            send_plane(n, k)

    inverse1 = inverse_cholesky(take_gram(gram_in, 0))
    left1 = full_dot(inverse1, left0)
    send_gram(gram_in2, 1, left1)

    send_z(0)
    send_z(1)

    gather_plane(0)
    gather_plane(1)

    inverse2 = inverse_cholesky(take_gram(gram_in2, 1))
    left2 = full_dot(inverse2, left1)[:, 0:ROWS]
    left_ref[...] = left2
    wide_ref[...] = jnp.transpose(stack_left(left2)).astype(BF16)
    mix = full_dot(inverse2, inverse1)
    mix = jnp.transpose(jnp.pad(mix, ((0, 96), (0, 96))))[0:RANK]
    mix = jnp.transpose(stack_left(mix)).astype(BF16)[0:RANK]

    def right_of(n, part):
        columns = slice(STREAMS[n][0], sum(STREAMS[n]))
        sums = jnp.concatenate([streams[n][3][part, s] for s in range(4)], axis=0)
        right_ref[part, :, columns] = dot(mix, stack_right(sums)) * (1.0 / DP)

    near = (0, 1, 3, 2)
    for n in range(2):
        full = streams[n][3]
        for kx in near:
            got = core * XS + lax.rem(x + XS - kx, XS)
            wait_bytes(full.at[0, pl.ds(0, YS if kx else YS - 1)], ag_recv.at[n, kx])
            remote(full.at[got], full.at[got], ac_send.at[n], ac_recv.at[n, kx], sibling).start()
    for n in range(2):
        for kx in near:
            right_of(n, core * XS + lax.rem(x + XS - kx, XS))
    for n in range(2):
        full = streams[n][3]
        for kx in near:
            wait_bytes(full.at[0], ac_recv.at[n, kx])
            right_of(n, (1 - core) * XS + lax.rem(x + XS - kx, XS))

    wait_bytes(left_y.at[pl.ds(0, YS - 1)], ly_send)
    wait_bytes(left_z.at[pl.ds(0, ZS - 1)], lz_send)
    for which in range(2):
        wait_bytes(gram_in.at[pl.ds(0, MP - 1)], gr_send.at[which])
    wait_bytes(left_other, lc_send)
    wait_bytes(other, oc_send)
    for n, (_, xy_in, z_in, full) in enumerate(streams):
        wait_bytes(xy_in, xy_send.at[n])
        wait_bytes(z_in.at[pl.ds(0, ZS - 1)], z_send.at[n])
        wait_bytes(xy_in, ag_send.at[n])
        wait_bytes(full.at[pl.ds(0, XS)], ac_send.at[n])


def run_exchange(gradients, errors, seeds):
    hbm = pl.BlockSpec(memory_space=pltpu.HBM)
    vmem = pl.BlockSpec(memory_space=pltpu.VMEM)
    dma = pltpu.SemaphoreType.DMA
    return pl.pallas_call(
        exchange,
        out_shape=(
            jax.ShapeDtypeStruct((PARTS, ROWS, WIDE), F32),
            jax.ShapeDtypeStruct((PARTS, RANK, WIDE), F32),
            jax.ShapeDtypeStruct((ROWS, 6 * RANK), BF16),
            jax.ShapeDtypeStruct((RANK, ROWS), F32),
        ),
        in_specs=[hbm, hbm, hbm],
        out_specs=(vmem,) * 4,
        scratch_shapes=[
            pltpu.VMEM((PARTS, ROWS, WIDE), BF16),
            pltpu.VMEM((PARTS, ROWS, WIDE), F32),
            pltpu.VMEM((RANK, COLS), jnp.int32),
            pltpu.VMEM((PARTS, 64, WIDE), BF16),
            pltpu.VMEM((PARTS, 2 * ROWS, WIDE), BF16),
            pltpu.VMEM((YS, ROW_TILES, 8, 128), F32),
            pltpu.VMEM((ZS, ROW_TILES, 8, 128), F32),
            pltpu.VMEM((ROW_TILES, 8, 128), F32),
            pltpu.VMEM((ROW_TILES, 8, 128), F32),
            pltpu.VMEM((XS, ROWS, WIDE), F32),
            pltpu.VMEM((XS, 2 * ROWS, WIDE), BF16),
            pltpu.VMEM((MP, 8, 128), F32),
            pltpu.VMEM((MP, 8, 128), F32),
            *(
                pltpu.VMEM(shape + (8, width), F32)
                for _, width in STREAMS
                for shape in ((XS, YS), (XS * YS - 1,), (ZS,), (PARTS, YS))
            ),
            dma((2, PARTS)),
            dma,
            dma, dma, dma, dma, dma((2,)), dma((2,)),
            dma, dma, dma, dma, dma((2,)), dma((2,)), dma((2,)), dma((2,)),
            dma((2,)), dma((2, XS)), dma((2,)), dma((2, XS)),
        ],
        compiler_params=pltpu.CompilerParams(
            collective_id=0, has_side_effects=True, vmem_limit_bytes=40 * 1024 * 1024
        ),
        cost_estimate=pl.CostEstimate(flops=10**9, bytes_accessed=8 * 10**6, transcendentals=0),
        name="exchange",
    )(*(pltpu.with_memory_space_constraint(v, pltpu.HBM) for v in (gradients, errors, seeds)))


def finish(
    both_ref, right_ref, wide_ref, left_ref, new_hbm, update_hbm, right_hbm, left_hbm,
    new_buf, update_buf, new_sem, update_sem, right_sem, left_sem,
):
    copies = [pltpu.make_async_copy(left_ref, left_hbm, left_sem)]
    copies[0].start()
    for part in range(PARTS):
        columns = pl.ds(part * WIDE, WIDE)
        approx = dot(wide_ref[...], stack_right(right_ref[part]))
        new_buf[part] = both_ref[part] - approx
        update_buf[part] = approx.astype(BF16)
        for copy in (
            pltpu.make_async_copy(new_buf.at[part], new_hbm.at[:, columns], new_sem.at[part]),
            pltpu.make_async_copy(update_buf.at[part], update_hbm.at[:, columns], update_sem.at[part]),
            pltpu.make_async_copy(right_ref.at[part], right_hbm.at[:, columns], right_sem.at[part]),
        ):
            copy.start()
            copies.append(copy)
    for copy in copies:
        copy.wait()


def run_finish(*operands):
    hbm = pl.BlockSpec(memory_space=pltpu.HBM)
    vmem = pl.BlockSpec(memory_space=pltpu.VMEM)
    dma = pltpu.SemaphoreType.DMA
    return pl.pallas_call(
        finish,
        out_shape=(
            jax.ShapeDtypeStruct((ROWS, COLS), F32),
            jax.ShapeDtypeStruct((ROWS, COLS), BF16),
            jax.ShapeDtypeStruct((RANK, COLS), F32),
            jax.ShapeDtypeStruct((RANK, ROWS), F32),
        ),
        in_specs=[vmem] * 4,
        out_specs=(hbm,) * 4,
        scratch_shapes=[
            pltpu.VMEM((PARTS, ROWS, WIDE), F32),
            pltpu.VMEM((PARTS, ROWS, WIDE), BF16),
            dma((PARTS,)), dma((PARTS,)), dma((PARTS,)), dma,
        ],
        compiler_params=pltpu.CompilerParams(vmem_limit_bytes=40 * 1024 * 1024),
        cost_estimate=pl.CostEstimate(flops=10**9, bytes_accessed=10**7, transcendentals=0),
        name="finish",
    )(*operands)


def local(gradients, errors, seed_table):
    new_errors, update, right, left = run_finish(*run_exchange(gradients[0], errors[0], seed_table.T))
    return (new_errors[None], update, right.T, left.T)


def solution(mesh):
    in_specs = (P("dp", "mp", None), P("dp", "mp", None), P())
    out_specs = (P("dp", "mp", None), P("mp", None), P(), P("mp", None))
    return jax.shard_map(local, mesh=mesh, in_specs=in_specs, out_specs=out_specs, check_vma=False)
```

```python
import jax
import jax.numpy as jnp
from jax import lax
from jax.experimental import pallas as pl
from jax.experimental.pallas import tpu as pltpu
from jax.sharding import PartitionSpec as P

MESH = pl.DeviceIdType.MESH
F32, BF16 = jnp.float32, jnp.bfloat16
HIGHEST = lax.Precision.HIGHEST

ROWS, COLS, RANK = 192, 5120, 32
DP, MP, XS, YS = 32, 8, 4, 4
PARTS = 8
WIDE = COLS // PARTS
ROW_TILES = 6
STREAMS = ((0, 256), (256, 384))
GROUPS = ((0, 1), (2, 3), (4, 5), (6,), (7,))
ZS = DP // YS
FAR_Z = (4, 3, 5, 2, 6, 1, 7, 0)
FAR = (2, 1, 3, 0)


def split(value, parts):
    out = []
    for _ in range(parts):
        piece = value.astype(BF16)
        out.append(piece)
        value = value - piece.astype(F32)
    return out


def dot(a, b):
    return jnp.dot(a, b, preferred_element_type=F32)


def full_dot(a, b, dims=((1,), (0,))):
    return lax.dot_general(a, b, (dims, ((), ())), precision=HIGHEST, preferred_element_type=F32)


def inverse_cholesky(gram):
    row_id = lax.broadcasted_iota(jnp.int32, (RANK, 128), 0)
    lane_id = lax.broadcasted_iota(jnp.int32, (RANK, 128), 1)
    table = jnp.concatenate([gram, jnp.zeros((RANK, 128 - RANK), F32)], axis=1)
    table = table + jnp.where(lane_id == row_id + RANK, 1.0, 0.0)
    blocks = [table[8 * i : 8 * i + 8] for i in range(4)]
    for j in range(RANK - 1):
        at, within = j // 8, j % 8
        columns = {i: jnp.broadcast_to(blocks[i][:, j : j + 1], (8, 128)) for i in range(at, 4)}
        row = blocks[at][within : within + 1] * (1.0 / columns[at][within : within + 1])
        columns[at] = jnp.where(row_id[0:8] > within, columns[at], 0.0)
        for i, column in columns.items():
            blocks[i] = blocks[i] - column * row
    table = jnp.concatenate(blocks, axis=0)
    pivots = jnp.sum(jnp.where(lane_id == row_id, table, 0.0), axis=1, keepdims=True)
    return table[:, RANK : 2 * RANK] / jnp.sqrt(pivots)


def pack(gram):
    return jnp.concatenate([gram[8 * s : 8 * s + 8, :] for s in range(4)], axis=1)


def unpack(tile):
    return jnp.concatenate([tile[:, 32 * s : 32 * s + 32] for s in range(4)], axis=0)


def stack_left(value):
    h, m, l = [p.astype(F32) for p in split(value, 3)]
    return jnp.concatenate([h, h, m, m, h, l], axis=0)


def stack_right(value):
    h, m, l = split(value, 3)
    return jnp.concatenate([h, m, h, m, l, h], axis=0)


def exchange(
    g_hbm, e_hbm, seed_hbm, both_ref, right_ref, wide_ref, left_ref,
    g_buf, e_buf, seed_buf, start, merged,
    left_y, left_z, left_mine, left_other, other, other_split,
    gram_in, gram_in2,
    own_a, xy_in_a, z_in_a, full_a,
    own_b, xy_in_b, z_in_b, full_b,
    load_sem, seed_sem,
    ly_send, ly_recv, lz_send, lz_recv, gr_send, gr_recv,
    lc_send, lc_recv, oc_send, oc_recv, xy_send, xy_recv, z_send, z_recv,
    ag_send, ag_recv, ac_send, ac_recv,
):
    me = lax.axis_index("dp")
    mp = lax.axis_index("mp")
    z, y = me // YS, me % YS
    x, core = mp // 2, mp % 2
    sibling = (me, x * 2 + 1 - core)

    def plane(kx, ky):
        return (z * YS + lax.rem(y + ky, YS), lax.rem(x + kx, XS) * 2 + core)

    def over_dp(dz, dy):
        return (lax.rem(z + dz, ZS) * YS + lax.rem(y + dy, YS), mp)

    barrier = pltpu.get_barrier_semaphore()
    seed_copy = pltpu.make_async_copy(seed_hbm, seed_buf, seed_sem)
    seed_copy.start()
    peers = [over_dp(dz, 0) for dz in FAR_Z[:-1]] + [plane(kx, ky) for kx in FAR[:3] for ky in FAR[:3]]
    peers += [over_dp(0, dy) for dy in FAR[:3]] + [(me, lax.rem(mp + k, MP)) for k in range(1, MP)]
    for peer in peers:
        pl.semaphore_signal(barrier, inc=1, device_id=peer, device_id_type=MESH)

    loads = []
    for i in range(PARTS):
        columns = pl.ds(i * WIDE, WIDE)
        pair = (
            pltpu.make_async_copy(g_hbm.at[:, columns], g_buf.at[i], load_sem.at[0, i]),
            pltpu.make_async_copy(e_hbm.at[:, columns], e_buf.at[i], load_sem.at[1, i]),
        )
        for copy in pair:
            copy.start()
        loads.append(pair)

    seed_copy.wait()
    seeds = seed_buf[...].astype(F32) * (1.0 / 1024.0)
    less = seeds - seeds[0:1, :]
    shorter = jnp.sum(less * less, axis=1, keepdims=True) < jnp.sum(seeds * seeds, axis=1, keepdims=True)
    first = lax.broadcasted_iota(jnp.int32, (RANK, 1), 0) == 0
    take = jnp.where(jnp.logical_and(shorter, jnp.logical_not(first)), 1.0, 0.0)
    seeds = seeds - take * seeds[0:1, :]
    high, low = split(seeds, 2)
    for i in range(PARTS):
        columns = slice(i * WIDE, (i + 1) * WIDE)
        start[i] = jnp.concatenate([high[:, columns], low[:, columns]], axis=0)

    def product(group):
        a = jnp.concatenate([merged[i] for i in group], axis=1)
        b = jnp.concatenate([start[i] for i in group], axis=1)
        return lax.dot_general(a, b, (((1,), (1,)), ((), ())), preferred_element_type=F32)

    total = jnp.zeros((2 * ROWS, 64), F32)
    for n, group in enumerate(GROUPS):
        for i in group:
            for copy in loads[i]:
                copy.wait()
        for i in group:
            both = g_buf[i].astype(F32) + e_buf[i]
            both_ref[i] = both
            upper, lower = split(both, 2)
            merged[i, 0:ROWS, :] = upper
            merged[i, ROWS : 2 * ROWS, :] = lower
        if n:
            total = total + product(GROUPS[n - 1])
    total = total + product(GROUPS[-1])
    left = total[0:ROWS] + total[ROWS : 2 * ROWS]
    turned = jnp.transpose(jnp.pad(left, ((0, 64), (0, 64))))
    left = (turned[0:RANK] + turned[RANK : 2 * RANK]) * 1.024
    for s in range(4):
        left_y[y, s] = left[8 * s : 8 * s + 8, 0:128]
    for s in range(2):
        rest = left[16 * s : 16 * s + 16, 128:256]
        left_y[y, 4 + s] = rest[0:8] + pltpu.roll(rest[8:16], 64, 1)

    pl.semaphore_wait(barrier, len(peers))

    def remote(src, dst, send, recv, device):
        return pltpu.make_async_remote_copy(
            src_ref=src, dst_ref=dst, send_sem=send, recv_sem=recv, device_id=device, device_id_type=MESH
        )

    def wait_bytes(ref, sem):
        pltpu.make_async_copy(ref, ref, sem).wait()

    for dy in FAR[:3]:
        remote(left_y.at[y], left_y.at[y], ly_send, ly_recv, over_dp(0, dy)).start()
    for k in FAR:
        part = (1 - core) * XS + lax.rem(x + k, XS)
        remote(both_ref.at[part], other.at[k], oc_send, oc_recv, sibling).start()
    wait_bytes(left_y.at[pl.ds(0, YS - 1)], ly_recv)
    left_z[z] = jnp.sum(left_y[...], axis=0)
    for dz in FAR_Z[:-1]:
        remote(left_z.at[z], left_z.at[z], lz_send, lz_recv, over_dp(dz, 0)).start()
    wait_bytes(other, oc_recv)
    for k in range(XS):
        upper, lower = split(other[k], 2)
        other_split[k, 0:ROWS, :] = upper
        other_split[k, ROWS : 2 * ROWS, :] = lower
    wait_bytes(left_z.at[pl.ds(0, ZS - 1)], lz_recv)
    left_mine[...] = jnp.sum(left_z[...], axis=0)
    remote(left_mine, left_other, lc_send, lc_recv, sibling).start()
    half = lax.broadcasted_iota(jnp.int32, (8, 128), 1) < 64

    def matrix(tiles):
        rest = [jnp.where(half, v, 0.0) for t in (4, 5) for v in (tiles[t], pltpu.roll(tiles[t], 64, 1))]
        return jnp.concatenate(
            [jnp.concatenate([tiles[s] for s in range(4)], axis=0), jnp.concatenate(rest, axis=0)], axis=1
        )

    left0 = matrix(left_mine)

    def send_gram(slots, which, value):
        slots[mp] = pack(full_dot(value, value, ((1,), (1,))))

        @pl.loop(1, MP)
        def _(k):
            remote(
                slots.at[mp], slots.at[mp], gr_send.at[which], gr_recv.at[which], (me, lax.rem(mp + k, MP))
            ).start()

    def take_gram(slots, which):
        wait_bytes(slots.at[pl.ds(0, MP - 1)], gr_recv.at[which])
        return unpack(jnp.sum(slots[...], axis=0))

    send_gram(gram_in, 0, left0)

    def pieces_of(left):
        rows = jnp.concatenate([p.astype(F32) for p in split(left[:, 0:ROWS], 3)], axis=0)
        return jnp.concatenate([rows, rows], axis=1).astype(BF16)

    pieces = pieces_of(left0)
    mine = core * XS + x
    streams = (
        (own_a, xy_in_a, z_in_a, full_a),
        (own_b, xy_in_b, z_in_b, full_b),
    )

    def right_part(rows, values, n):
        value = dot(rows, values[:, STREAMS[n][0] : sum(STREAMS[n])])
        return value[0:32] + (value[32:64] + value[64:96])

    def put(into, value, more):
        for s in range(YS):
            piece = value[8 * s : 8 * s + 8]
            into[s] = into[s] + piece if more else piece

    def my_rows(n, k):
        return right_part(pieces, merged.at[core * XS + lax.rem(x + k, XS)], n)

    def send_plane(n, kx):
        own, xy_in = streams[n][0:2]
        for ky in FAR:
            if kx or ky:
                remote(
                    own.at[kx, lax.rem(y + ky, YS)], xy_in.at[kx * YS + ky - 1],
                    xy_send.at[n], xy_recv.at[n], plane(kx, ky),
                ).start()

    def send_z(n):
        own, xy_in, z_in = streams[n][0:3]
        wait_bytes(xy_in, xy_recv.at[n])
        z_in[z] = own[0, y] + jnp.sum(xy_in[...], axis=0)
        for dz in FAR_Z[:-1]:
            remote(z_in.at[z], z_in.at[z], z_send.at[n], z_recv.at[n], over_dp(dz, 0)).start()

    def gather_plane(n):
        z_in, full = streams[n][2:4]
        wait_bytes(z_in.at[pl.ds(0, ZS - 1)], z_recv.at[n])
        full[mine, y] = jnp.sum(z_in[...], axis=0)
        for kx in FAR:
            for ky in FAR:
                if kx or ky:
                    remote(
                        full.at[mine, y], full.at[mine, y], ag_send.at[n], ag_recv.at[n, kx], plane(kx, ky)
                    ).start()

    for k in FAR:
        put(own_a.at[k], my_rows(0, k), False)
    wait_bytes(left_other, lc_recv)
    pieces_other = pieces_of(matrix(left_other))
    for n in range(2):
        for k in FAR:
            value = right_part(pieces_other, other_split.at[k], n)
            if n:
                value = value + my_rows(n, k)
            put(streams[n][0].at[k], value, n == 0)
            send_plane(n, k)

    inverse1 = inverse_cholesky(take_gram(gram_in, 0))
    left1 = full_dot(inverse1, left0)
    send_gram(gram_in2, 1, left1)

    send_z(0)
    send_z(1)

    gather_plane(0)
    gather_plane(1)

    inverse2 = inverse_cholesky(take_gram(gram_in2, 1))
    left2 = full_dot(inverse2, left1)[:, 0:ROWS]
    left_ref[...] = left2
    wide_ref[...] = jnp.transpose(stack_left(left2)).astype(BF16)
    mix = full_dot(inverse2, inverse1)
    mix = jnp.transpose(jnp.pad(mix, ((0, 96), (0, 96))))[0:RANK]
    mix = jnp.transpose(stack_left(mix)).astype(BF16)[0:RANK]

    def right_of(n, part):
        columns = slice(STREAMS[n][0], sum(STREAMS[n]))
        sums = jnp.concatenate([streams[n][3][part, s] for s in range(4)], axis=0)
        right_ref[part, :, columns] = dot(mix, stack_right(sums)) * (1.0 / DP)

    near = (0, 1, 3, 2)
    for n in range(2):
        full = streams[n][3]
        for kx in near:
            got = core * XS + lax.rem(x + XS - kx, XS)
            wait_bytes(full.at[0, pl.ds(0, YS if kx else YS - 1)], ag_recv.at[n, kx])
            remote(full.at[got], full.at[got], ac_send.at[n], ac_recv.at[n, kx], sibling).start()
    for n in range(2):
        for kx in near:
            right_of(n, core * XS + lax.rem(x + XS - kx, XS))
    for n in range(2):
        full = streams[n][3]
        for kx in near:
            wait_bytes(full.at[0], ac_recv.at[n, kx])
            right_of(n, (1 - core) * XS + lax.rem(x + XS - kx, XS))

    wait_bytes(left_y.at[pl.ds(0, YS - 1)], ly_send)
    wait_bytes(left_z.at[pl.ds(0, ZS - 1)], lz_send)
    for which in range(2):
        wait_bytes(gram_in.at[pl.ds(0, MP - 1)], gr_send.at[which])
    wait_bytes(left_other, lc_send)
    wait_bytes(other, oc_send)
    for n, (_, xy_in, z_in, full) in enumerate(streams):
        wait_bytes(xy_in, xy_send.at[n])
        wait_bytes(z_in.at[pl.ds(0, ZS - 1)], z_send.at[n])
        wait_bytes(xy_in, ag_send.at[n])
        wait_bytes(full.at[pl.ds(0, XS)], ac_send.at[n])


def run_exchange(gradients, errors, seeds):
    hbm = pl.BlockSpec(memory_space=pltpu.HBM)
    vmem = pl.BlockSpec(memory_space=pltpu.VMEM)
    dma = pltpu.SemaphoreType.DMA
    return pl.pallas_call(
        exchange,
        out_shape=(
            jax.ShapeDtypeStruct((PARTS, ROWS, WIDE), F32),
            jax.ShapeDtypeStruct((PARTS, RANK, WIDE), F32),
            jax.ShapeDtypeStruct((ROWS, 6 * RANK), BF16),
            jax.ShapeDtypeStruct((RANK, ROWS), F32),
        ),
        in_specs=[hbm, hbm, hbm],
        out_specs=(vmem,) * 4,
        scratch_shapes=[
            pltpu.VMEM((PARTS, ROWS, WIDE), BF16),
            pltpu.VMEM((PARTS, ROWS, WIDE), F32),
            pltpu.VMEM((RANK, COLS), jnp.int32),
            pltpu.VMEM((PARTS, 64, WIDE), BF16),
            pltpu.VMEM((PARTS, 2 * ROWS, WIDE), BF16),
            pltpu.VMEM((YS, ROW_TILES, 8, 128), F32),
            pltpu.VMEM((ZS, ROW_TILES, 8, 128), F32),
            pltpu.VMEM((ROW_TILES, 8, 128), F32),
            pltpu.VMEM((ROW_TILES, 8, 128), F32),
            pltpu.VMEM((XS, ROWS, WIDE), F32),
            pltpu.VMEM((XS, 2 * ROWS, WIDE), BF16),
            pltpu.VMEM((MP, 8, 128), F32),
            pltpu.VMEM((MP, 8, 128), F32),
            *(
                pltpu.VMEM(shape + (8, width), F32)
                for _, width in STREAMS
                for shape in ((XS, YS), (XS * YS - 1,), (ZS,), (PARTS, YS))
            ),
            dma((2, PARTS)),
            dma,
            dma, dma, dma, dma, dma((2,)), dma((2,)),
            dma, dma, dma, dma, dma((2,)), dma((2,)), dma((2,)), dma((2,)),
            dma((2,)), dma((2, XS)), dma((2,)), dma((2, XS)),
        ],
        compiler_params=pltpu.CompilerParams(
            collective_id=0, has_side_effects=True, vmem_limit_bytes=40 * 1024 * 1024
        ),
        cost_estimate=pl.CostEstimate(flops=10**9, bytes_accessed=8 * 10**6, transcendentals=0),
        name="exchange",
    )(*(pltpu.with_memory_space_constraint(v, pltpu.HBM) for v in (gradients, errors, seeds)))


def finish(
    both_ref, right_ref, wide_ref, left_ref, new_hbm, update_hbm, right_hbm, left_hbm,
    new_buf, update_buf, new_sem, update_sem, right_sem, left_sem,
):
    copies = [pltpu.make_async_copy(left_ref, left_hbm, left_sem)]
    copies[0].start()
    for part in range(PARTS):
        columns = pl.ds(part * WIDE, WIDE)
        approx = dot(wide_ref[...], stack_right(right_ref[part]))
        new_buf[part] = both_ref[part] - approx
        update_buf[part] = approx.astype(BF16)
        for copy in (
            pltpu.make_async_copy(new_buf.at[part], new_hbm.at[:, columns], new_sem.at[part]),
            pltpu.make_async_copy(update_buf.at[part], update_hbm.at[:, columns], update_sem.at[part]),
            pltpu.make_async_copy(right_ref.at[part], right_hbm.at[:, columns], right_sem.at[part]),
        ):
            copy.start()
            copies.append(copy)
    for copy in copies:
        copy.wait()


def run_finish(*operands):
    hbm = pl.BlockSpec(memory_space=pltpu.HBM)
    vmem = pl.BlockSpec(memory_space=pltpu.VMEM)
    dma = pltpu.SemaphoreType.DMA
    return pl.pallas_call(
        finish,
        out_shape=(
            jax.ShapeDtypeStruct((ROWS, COLS), F32),
            jax.ShapeDtypeStruct((ROWS, COLS), BF16),
            jax.ShapeDtypeStruct((RANK, COLS), F32),
            jax.ShapeDtypeStruct((RANK, ROWS), F32),
        ),
        in_specs=[vmem] * 4,
        out_specs=(hbm,) * 4,
        scratch_shapes=[
            pltpu.VMEM((PARTS, ROWS, WIDE), F32),
            pltpu.VMEM((PARTS, ROWS, WIDE), BF16),
            dma((PARTS,)), dma((PARTS,)), dma((PARTS,)), dma,
        ],
        compiler_params=pltpu.CompilerParams(vmem_limit_bytes=40 * 1024 * 1024),
        cost_estimate=pl.CostEstimate(flops=10**9, bytes_accessed=10**7, transcendentals=0),
        name="finish",
    )(*operands)


def local(gradients, errors, seed_table):
    new_errors, update, right, left = run_finish(*run_exchange(gradients[0], errors[0], seed_table.T))
    return (new_errors[None], update, right.T, left.T)


def solution(mesh):
    in_specs = (P("dp", "mp", None), P("dp", "mp", None), P())
    out_specs = (P("dp", "mp", None), P("mp", None), P(), P("mp", None))
    return jax.shard_map(local, mesh=mesh, in_specs=in_specs, out_specs=out_specs, check_vma=False)
```

```python
import jax
import jax.numpy as jnp
from jax import lax
from jax.experimental import pallas as pl
from jax.experimental.pallas import tpu as pltpu
from jax.sharding import PartitionSpec as P

MESH = pl.DeviceIdType.MESH
F32, BF16 = jnp.float32, jnp.bfloat16
HIGHEST = lax.Precision.HIGHEST

ROWS, COLS, RANK = 192, 5120, 32
DP, MP, XS, YS = 32, 8, 4, 4
PARTS = 8
WIDE = COLS // PARTS
ROW_TILES = 6
STREAMS = ((0, 128), (128, 512))
GROUPS = ((0, 1), (2, 3), (4, 5), (6,), (7,))
ZS = DP // YS
FAR_Z = (4, 3, 5, 2, 6, 1, 7, 0)
FAR = (2, 1, 3, 0)


def split(value, parts):
    out = []
    for _ in range(parts):
        piece = value.astype(BF16)
        out.append(piece)
        value = value - piece.astype(F32)
    return out


def dot(a, b):
    return jnp.dot(a, b, preferred_element_type=F32)


def full_dot(a, b, dims=((1,), (0,))):
    return lax.dot_general(a, b, (dims, ((), ())), precision=HIGHEST, preferred_element_type=F32)


def inverse_cholesky(gram):
    row_id = lax.broadcasted_iota(jnp.int32, (RANK, 128), 0)
    lane_id = lax.broadcasted_iota(jnp.int32, (RANK, 128), 1)
    table = jnp.concatenate([gram, jnp.zeros((RANK, 128 - RANK), F32)], axis=1)
    table = table + jnp.where(lane_id == row_id + RANK, 1.0, 0.0)
    blocks = [table[8 * i : 8 * i + 8] for i in range(4)]
    for j in range(RANK - 1):
        at, within = j // 8, j % 8
        columns = {i: jnp.broadcast_to(blocks[i][:, j : j + 1], (8, 128)) for i in range(at, 4)}
        row = blocks[at][within : within + 1] * (1.0 / columns[at][within : within + 1])
        columns[at] = jnp.where(row_id[0:8] > within, columns[at], 0.0)
        for i, column in columns.items():
            blocks[i] = blocks[i] - column * row
    table = jnp.concatenate(blocks, axis=0)
    pivots = jnp.sum(jnp.where(lane_id == row_id, table, 0.0), axis=1, keepdims=True)
    return table[:, RANK : 2 * RANK] / jnp.sqrt(pivots)


def pack(gram):
    return jnp.concatenate([gram[8 * s : 8 * s + 8, :] for s in range(4)], axis=1)


def unpack(tile):
    return jnp.concatenate([tile[:, 32 * s : 32 * s + 32] for s in range(4)], axis=0)


def stack_left(value):
    h, m, l = [p.astype(F32) for p in split(value, 3)]
    return jnp.concatenate([h, h, m, m, h, l], axis=0)


def stack_right(value):
    h, m, l = split(value, 3)
    return jnp.concatenate([h, m, h, m, l, h], axis=0)


def exchange(
    g_hbm, e_hbm, seed_hbm, both_ref, right_ref, wide_ref, left_ref,
    g_buf, e_buf, seed_buf, start, merged,
    left_y, left_z, left_mine, left_other, other, other_split,
    gram_in, gram_in2,
    own_a, xy_in_a, z_in_a, full_a,
    own_b, xy_in_b, z_in_b, full_b,
    load_sem, seed_sem,
    ly_send, ly_recv, lz_send, lz_recv, gr_send, gr_recv,
    lc_send, lc_recv, oc_send, oc_recv, xy_send, xy_recv, z_send, z_recv,
    ag_send, ag_recv, ac_send, ac_recv,
):
    me = lax.axis_index("dp")
    mp = lax.axis_index("mp")
    z, y = me // YS, me % YS
    x, core = mp // 2, mp % 2
    sibling = (me, x * 2 + 1 - core)

    def plane(kx, ky):
        return (z * YS + lax.rem(y + ky, YS), lax.rem(x + kx, XS) * 2 + core)

    def over_dp(dz, dy):
        return (lax.rem(z + dz, ZS) * YS + lax.rem(y + dy, YS), mp)

    barrier = pltpu.get_barrier_semaphore()
    seed_copy = pltpu.make_async_copy(seed_hbm, seed_buf, seed_sem)
    seed_copy.start()
    peers = [over_dp(dz, 0) for dz in FAR_Z[:-1]] + [plane(kx, ky) for kx in FAR[:3] for ky in FAR[:3]]
    peers += [over_dp(0, dy) for dy in FAR[:3]] + [(me, lax.rem(mp + k, MP)) for k in range(1, MP)]
    for peer in peers:
        pl.semaphore_signal(barrier, inc=1, device_id=peer, device_id_type=MESH)

    loads = []
    for i in range(PARTS):
        columns = pl.ds(i * WIDE, WIDE)
        pair = (
            pltpu.make_async_copy(g_hbm.at[:, columns], g_buf.at[i], load_sem.at[0, i]),
            pltpu.make_async_copy(e_hbm.at[:, columns], e_buf.at[i], load_sem.at[1, i]),
        )
        for copy in pair:
            copy.start()
        loads.append(pair)

    seed_copy.wait()
    seeds = seed_buf[...].astype(F32) * (1.0 / 1024.0)
    less = seeds - seeds[0:1, :]
    shorter = jnp.sum(less * less, axis=1, keepdims=True) < jnp.sum(seeds * seeds, axis=1, keepdims=True)
    first = lax.broadcasted_iota(jnp.int32, (RANK, 1), 0) == 0
    take = jnp.where(jnp.logical_and(shorter, jnp.logical_not(first)), 1.0, 0.0)
    seeds = seeds - take * seeds[0:1, :]
    high, low = split(seeds, 2)
    for i in range(PARTS):
        columns = slice(i * WIDE, (i + 1) * WIDE)
        start[i] = jnp.concatenate([high[:, columns], low[:, columns]], axis=0)

    def product(group):
        a = jnp.concatenate([merged[i] for i in group], axis=1)
        b = jnp.concatenate([start[i] for i in group], axis=1)
        return lax.dot_general(a, b, (((1,), (1,)), ((), ())), preferred_element_type=F32)

    total = jnp.zeros((2 * ROWS, 64), F32)
    for n, group in enumerate(GROUPS):
        for i in group:
            for copy in loads[i]:
                copy.wait()
        for i in group:
            both = g_buf[i].astype(F32) + e_buf[i]
            both_ref[i] = both
            upper, lower = split(both, 2)
            merged[i, 0:ROWS, :] = upper
            merged[i, ROWS : 2 * ROWS, :] = lower
        if n:
            total = total + product(GROUPS[n - 1])
    total = total + product(GROUPS[-1])
    left = total[0:ROWS] + total[ROWS : 2 * ROWS]
    turned = jnp.transpose(jnp.pad(left, ((0, 64), (0, 64))))
    left = (turned[0:RANK] + turned[RANK : 2 * RANK]) * 1.024
    for s in range(4):
        left_y[y, s] = left[8 * s : 8 * s + 8, 0:128]
    for s in range(2):
        rest = left[16 * s : 16 * s + 16, 128:256]
        left_y[y, 4 + s] = rest[0:8] + pltpu.roll(rest[8:16], 64, 1)

    pl.semaphore_wait(barrier, len(peers))

    def remote(src, dst, send, recv, device):
        return pltpu.make_async_remote_copy(
            src_ref=src, dst_ref=dst, send_sem=send, recv_sem=recv, device_id=device, device_id_type=MESH
        )

    def wait_bytes(ref, sem):
        pltpu.make_async_copy(ref, ref, sem).wait()

    for dy in FAR[:3]:
        remote(left_y.at[y], left_y.at[y], ly_send, ly_recv, over_dp(0, dy)).start()
    for k in FAR:
        part = (1 - core) * XS + lax.rem(x + k, XS)
        remote(both_ref.at[part], other.at[k], oc_send, oc_recv, sibling).start()
    wait_bytes(left_y.at[pl.ds(0, YS - 1)], ly_recv)
    left_z[z] = jnp.sum(left_y[...], axis=0)
    for dz in FAR_Z[:-1]:
        remote(left_z.at[z], left_z.at[z], lz_send, lz_recv, over_dp(dz, 0)).start()
    wait_bytes(other, oc_recv)
    for k in range(XS):
        upper, lower = split(other[k], 2)
        other_split[k, 0:ROWS, :] = upper
        other_split[k, ROWS : 2 * ROWS, :] = lower
    wait_bytes(left_z.at[pl.ds(0, ZS - 1)], lz_recv)
    left_mine[...] = jnp.sum(left_z[...], axis=0)
    remote(left_mine, left_other, lc_send, lc_recv, sibling).start()
    half = lax.broadcasted_iota(jnp.int32, (8, 128), 1) < 64

    def matrix(tiles):
        rest = [jnp.where(half, v, 0.0) for t in (4, 5) for v in (tiles[t], pltpu.roll(tiles[t], 64, 1))]
        return jnp.concatenate(
            [jnp.concatenate([tiles[s] for s in range(4)], axis=0), jnp.concatenate(rest, axis=0)], axis=1
        )

    left0 = matrix(left_mine)

    def send_gram(slots, which, value):
        slots[mp] = pack(full_dot(value, value, ((1,), (1,))))

        @pl.loop(1, MP)
        def _(k):
            remote(
                slots.at[mp], slots.at[mp], gr_send.at[which], gr_recv.at[which], (me, lax.rem(mp + k, MP))
            ).start()

    def take_gram(slots, which):
        wait_bytes(slots.at[pl.ds(0, MP - 1)], gr_recv.at[which])
        return unpack(jnp.sum(slots[...], axis=0))

    send_gram(gram_in, 0, left0)

    def pieces_of(left):
        rows = jnp.concatenate([p.astype(F32) for p in split(left[:, 0:ROWS], 3)], axis=0)
        return jnp.concatenate([rows, rows], axis=1).astype(BF16)

    pieces = pieces_of(left0)
    mine = core * XS + x
    streams = (
        (own_a, xy_in_a, z_in_a, full_a),
        (own_b, xy_in_b, z_in_b, full_b),
    )

    def right_part(rows, values, n):
        value = dot(rows, values[:, STREAMS[n][0] : sum(STREAMS[n])])
        return value[0:32] + (value[32:64] + value[64:96])

    def put(into, value, more):
        for s in range(YS):
            piece = value[8 * s : 8 * s + 8]
            into[s] = into[s] + piece if more else piece

    def my_rows(n, k):
        return right_part(pieces, merged.at[core * XS + lax.rem(x + k, XS)], n)

    def send_plane(n, kx):
        own, xy_in = streams[n][0:2]
        for ky in FAR:
            if kx or ky:
                remote(
                    own.at[kx, lax.rem(y + ky, YS)], xy_in.at[kx * YS + ky - 1],
                    xy_send.at[n], xy_recv.at[n], plane(kx, ky),
                ).start()

    def send_z(n):
        own, xy_in, z_in = streams[n][0:3]
        wait_bytes(xy_in, xy_recv.at[n])
        z_in[z] = own[0, y] + jnp.sum(xy_in[...], axis=0)
        for dz in FAR_Z[:-1]:
            remote(z_in.at[z], z_in.at[z], z_send.at[n], z_recv.at[n], over_dp(dz, 0)).start()

    def gather_plane(n):
        z_in, full = streams[n][2:4]
        wait_bytes(z_in.at[pl.ds(0, ZS - 1)], z_recv.at[n])
        full[mine, y] = jnp.sum(z_in[...], axis=0)
        for kx in FAR:
            for ky in FAR:
                if kx or ky:
                    remote(
                        full.at[mine, y], full.at[mine, y], ag_send.at[n], ag_recv.at[n, kx], plane(kx, ky)
                    ).start()

    for k in FAR:
        put(own_a.at[k], my_rows(0, k), False)
    wait_bytes(left_other, lc_recv)
    pieces_other = pieces_of(matrix(left_other))
    for n in range(2):
        for k in FAR:
            value = right_part(pieces_other, other_split.at[k], n)
            if n:
                value = value + my_rows(n, k)
            put(streams[n][0].at[k], value, n == 0)
            send_plane(n, k)

    inverse1 = inverse_cholesky(take_gram(gram_in, 0))
    left1 = full_dot(inverse1, left0)
    send_gram(gram_in2, 1, left1)

    send_z(0)
    send_z(1)

    gather_plane(0)
    gather_plane(1)

    inverse2 = inverse_cholesky(take_gram(gram_in2, 1))
    left2 = full_dot(inverse2, left1)[:, 0:ROWS]
    left_ref[...] = left2
    wide_ref[...] = jnp.transpose(stack_left(left2)).astype(BF16)
    mix = full_dot(inverse2, inverse1)
    mix = jnp.transpose(jnp.pad(mix, ((0, 96), (0, 96))))[0:RANK]
    mix = jnp.transpose(stack_left(mix)).astype(BF16)[0:RANK]

    def right_of(n, part):
        columns = slice(STREAMS[n][0], sum(STREAMS[n]))
        sums = jnp.concatenate([streams[n][3][part, s] for s in range(4)], axis=0)
        right_ref[part, :, columns] = dot(mix, stack_right(sums)) * (1.0 / DP)

    near = (0, 1, 3, 2)
    for n in range(2):
        full = streams[n][3]
        for kx in near:
            got = core * XS + lax.rem(x + XS - kx, XS)
            wait_bytes(full.at[0, pl.ds(0, YS if kx else YS - 1)], ag_recv.at[n, kx])
            remote(full.at[got], full.at[got], ac_send.at[n], ac_recv.at[n, kx], sibling).start()
    for n in range(2):
        for kx in near:
            right_of(n, core * XS + lax.rem(x + XS - kx, XS))
    for n in range(2):
        full = streams[n][3]
        for kx in near:
            wait_bytes(full.at[0], ac_recv.at[n, kx])
            right_of(n, (1 - core) * XS + lax.rem(x + XS - kx, XS))

    wait_bytes(left_y.at[pl.ds(0, YS - 1)], ly_send)
    wait_bytes(left_z.at[pl.ds(0, ZS - 1)], lz_send)
    for which in range(2):
        wait_bytes(gram_in.at[pl.ds(0, MP - 1)], gr_send.at[which])
    wait_bytes(left_other, lc_send)
    wait_bytes(other, oc_send)
    for n, (_, xy_in, z_in, full) in enumerate(streams):
        wait_bytes(xy_in, xy_send.at[n])
        wait_bytes(z_in.at[pl.ds(0, ZS - 1)], z_send.at[n])
        wait_bytes(xy_in, ag_send.at[n])
        wait_bytes(full.at[pl.ds(0, XS)], ac_send.at[n])


def run_exchange(gradients, errors, seeds):
    hbm = pl.BlockSpec(memory_space=pltpu.HBM)
    vmem = pl.BlockSpec(memory_space=pltpu.VMEM)
    dma = pltpu.SemaphoreType.DMA
    return pl.pallas_call(
        exchange,
        out_shape=(
            jax.ShapeDtypeStruct((PARTS, ROWS, WIDE), F32),
            jax.ShapeDtypeStruct((PARTS, RANK, WIDE), F32),
            jax.ShapeDtypeStruct((ROWS, 6 * RANK), BF16),
            jax.ShapeDtypeStruct((RANK, ROWS), F32),
        ),
        in_specs=[hbm, hbm, hbm],
        out_specs=(vmem,) * 4,
        scratch_shapes=[
            pltpu.VMEM((PARTS, ROWS, WIDE), BF16),
            pltpu.VMEM((PARTS, ROWS, WIDE), F32),
            pltpu.VMEM((RANK, COLS), jnp.int32),
            pltpu.VMEM((PARTS, 64, WIDE), BF16),
            pltpu.VMEM((PARTS, 2 * ROWS, WIDE), BF16),
            pltpu.VMEM((YS, ROW_TILES, 8, 128), F32),
            pltpu.VMEM((ZS, ROW_TILES, 8, 128), F32),
            pltpu.VMEM((ROW_TILES, 8, 128), F32),
            pltpu.VMEM((ROW_TILES, 8, 128), F32),
            pltpu.VMEM((XS, ROWS, WIDE), F32),
            pltpu.VMEM((XS, 2 * ROWS, WIDE), BF16),
            pltpu.VMEM((MP, 8, 128), F32),
            pltpu.VMEM((MP, 8, 128), F32),
            *(
                pltpu.VMEM(shape + (8, width), F32)
                for _, width in STREAMS
                for shape in ((XS, YS), (XS * YS - 1,), (ZS,), (PARTS, YS))
            ),
            dma((2, PARTS)),
            dma,
            dma, dma, dma, dma, dma((2,)), dma((2,)),
            dma, dma, dma, dma, dma((2,)), dma((2,)), dma((2,)), dma((2,)),
            dma((2,)), dma((2, XS)), dma((2,)), dma((2, XS)),
        ],
        compiler_params=pltpu.CompilerParams(
            collective_id=0, has_side_effects=True, vmem_limit_bytes=40 * 1024 * 1024
        ),
        cost_estimate=pl.CostEstimate(flops=10**9, bytes_accessed=8 * 10**6, transcendentals=0),
        name="exchange",
    )(*(pltpu.with_memory_space_constraint(v, pltpu.HBM) for v in (gradients, errors, seeds)))


def finish(
    both_ref, right_ref, wide_ref, left_ref, new_hbm, update_hbm, right_hbm, left_hbm,
    new_buf, update_buf, new_sem, update_sem, right_sem, left_sem,
):
    copies = [pltpu.make_async_copy(left_ref, left_hbm, left_sem)]
    copies[0].start()
    for part in range(PARTS):
        columns = pl.ds(part * WIDE, WIDE)
        approx = dot(wide_ref[...], stack_right(right_ref[part]))
        new_buf[part] = both_ref[part] - approx
        update_buf[part] = approx.astype(BF16)
        for copy in (
            pltpu.make_async_copy(new_buf.at[part], new_hbm.at[:, columns], new_sem.at[part]),
            pltpu.make_async_copy(update_buf.at[part], update_hbm.at[:, columns], update_sem.at[part]),
            pltpu.make_async_copy(right_ref.at[part], right_hbm.at[:, columns], right_sem.at[part]),
        ):
            copy.start()
            copies.append(copy)
    for copy in copies:
        copy.wait()


def run_finish(*operands):
    hbm = pl.BlockSpec(memory_space=pltpu.HBM)
    vmem = pl.BlockSpec(memory_space=pltpu.VMEM)
    dma = pltpu.SemaphoreType.DMA
    return pl.pallas_call(
        finish,
        out_shape=(
            jax.ShapeDtypeStruct((ROWS, COLS), F32),
            jax.ShapeDtypeStruct((ROWS, COLS), BF16),
            jax.ShapeDtypeStruct((RANK, COLS), F32),
            jax.ShapeDtypeStruct((RANK, ROWS), F32),
        ),
        in_specs=[vmem] * 4,
        out_specs=(hbm,) * 4,
        scratch_shapes=[
            pltpu.VMEM((PARTS, ROWS, WIDE), F32),
            pltpu.VMEM((PARTS, ROWS, WIDE), BF16),
            dma((PARTS,)), dma((PARTS,)), dma((PARTS,)), dma,
        ],
        compiler_params=pltpu.CompilerParams(vmem_limit_bytes=40 * 1024 * 1024),
        cost_estimate=pl.CostEstimate(flops=10**9, bytes_accessed=10**7, transcendentals=0),
        name="finish",
    )(*operands)


def local(gradients, errors, seed_table):
    new_errors, update, right, left = run_finish(*run_exchange(gradients[0], errors[0], seed_table.T))
    return (new_errors[None], update, right.T, left.T)


def solution(mesh):
    in_specs = (P("dp", "mp", None), P("dp", "mp", None), P())
    out_specs = (P("dp", "mp", None), P("mp", None), P(), P("mp", None))
    return jax.shard_map(local, mesh=mesh, in_specs=in_specs, out_specs=out_specs, check_vma=False)
```
